512 devices in a mesh: outer: 32 (over z_lo, x), inner: 16 (over y, z_hi, core).
Axes of the slice: x: 4, y: 4, z: 16 (z_hi: 2, z_lo: 8; z = z_hi * 8 + z_lo), core: 2. Of those that a mesh axis runs over, the one named last changes fastest.
Arguments:
- queries: bfloat16 [131072, 768], P(('outer', 'inner')), may hold values from -18 to 18
- keys: bfloat16 [131072, 768], P(('outer', 'inner')), may hold values from -6 to 6
- values: bfloat16 [131072, 768], P(('outer', 'inner')), may hold values from -6 to 6
Outputs:
- attended: bfloat16 [131072, 768], P(('outer', 'inner'))
The draws below stay inside these ranges and needn't reach their ends.
All inputs are finite; a program needn't handle non-finite values.
Results may differ from the reference program's by a relative error of at most 0.0065.
Values may be sent and summed in bfloat16 or wider, within the bound.
No kernel may reach another device: no remote copies, remote signals or barrier semaphores. Data moves between devices by JAX's collectives and lax.ppermute only.
A program may use at most 128 MiB of HBM per device.

```python
import jax
import jax.numpy as jnp
import numpy as np
from jax import lax

WIDTH = 768
HEADS = 12
HEAD_DIM = 64
R3 = 128
SEGMENT = 4096
TOKENS = 131072


def draw_queries(key, part):
    key = jax.random.fold_in(key, 1)
    drawn = 3.0 * jax.random.truncated_normal(key, -6.0, 6.0, (TOKENS, WIDTH), jnp.float32)
    return drawn.astype(jnp.bfloat16)


def draw_keys(key, part):
    key = jax.random.fold_in(key, 2)
    drawn = jax.random.truncated_normal(key, -6.0, 6.0, (TOKENS, WIDTH), jnp.float32)
    return drawn.astype(jnp.bfloat16)


def levels(own_key, extent, shards, smallest, top_value):
    def one(dim, parts):
        draws = jax.random.uniform(jax.random.fold_in(jax.random.fold_in(own_key, 6), dim), (parts,), jnp.float32, smallest / len(shards), top_value / len(shards))
        return jnp.repeat(jnp.exp(draws), extent[dim] // parts).reshape((-1,) + (1,) * (len(extent) - dim - 1))

    level = one(*shards[0])
    for cut in shards[1:]:
        level = level * one(*cut)
    return level


def centred(key, extent, deviation, limit, shards=(), dtype=jnp.bfloat16):
    factor_of = levels(key, extent, shards, -0.22, 0.18) if shards else 1.0
    entries = jax.random.normal(key, extent, jnp.float32) * deviation * factor_of
    return jnp.minimum(jnp.maximum(entries, -limit), limit).astype(dtype)


def setup_inputs(seed: int = 0) -> dict:
    splits = jax.random.split(jax.random.key(seed), 4)
    return {
        "queries": draw_queries(jax.random.fold_in(splits[3], 71), 0),
        "keys": draw_keys(jax.random.fold_in(splits[3], 71), 0),
        "values": centred(splits[2], (TOKENS, WIDTH), 1.0, 6.0, ((0, 512),)),
    }


def select(rows, dilation):
    count = rows.shape[0]
    shaped = rows.reshape(count // dilation, dilation, HEADS, HEAD_DIM)
    return shaped[:, np.arange(HEADS) % dilation, np.arange(HEADS), :]


def attend_one(operands):
    query_rows, key_rows, value_rows = operands
    scores = jnp.einsum("nd,md->nm", query_rows.astype(jnp.float32), key_rows.astype(jnp.float32)) * (HEAD_DIM ** -0.5)
    peak = jnp.max(scores, axis=-1)
    expos = jnp.exp(scores - peak[:, None])
    total = jnp.sum(expos, axis=-1)
    weight = expos.astype(jnp.bfloat16)
    partial_value = jnp.einsum("nm,md->nd", weight.astype(jnp.float32), value_rows.astype(jnp.float32))
    return peak, total, partial_value


def attend_heads(query_rows, key_rows, value_rows):
    return lax.map(attend_one, (query_rows.transpose(1, 0, 2), key_rows.transpose(1, 0, 2),
                                value_rows.transpose(1, 0, 2)))


def combine(first, second):
    peak = jnp.maximum(first[0], second[0])
    scale_one = jnp.exp(first[0] - peak)
    scale_two = jnp.exp(second[0] - peak)
    return (peak, first[1] * scale_one + second[1] * scale_two,
            first[2] * scale_one[..., None] + second[2] * scale_two[..., None])


def merge_into(state, level, dilation):
    peak, total, partial_value = state
    count = peak.shape[1]
    heads = np.arange(HEADS)
    offsets = heads % dilation
    peak_view = peak.reshape(HEADS, count // dilation, dilation)
    total_view = total.reshape(HEADS, count // dilation, dilation)
    sum_view = partial_value.reshape(HEADS, count // dilation, dilation, HEAD_DIM)
    merged = combine((peak_view[heads, :, offsets], total_view[heads, :, offsets], sum_view[heads, :, offsets]), level)
    peak_view = peak_view.at[heads, :, offsets].set(merged[0])
    total_view = total_view.at[heads, :, offsets].set(merged[1])
    sum_view = sum_view.at[heads, :, offsets].set(merged[2])
    return (peak_view.reshape(HEADS, count), total_view.reshape(HEADS, count), sum_view.reshape(HEADS, count, HEAD_DIM))


def one_segment(operands):
    return attend_heads(operands[0], operands[1], operands[2])


def reference(queries, keys, values):
    query_heads = queries.reshape(TOKENS, HEADS, HEAD_DIM)
    key_heads = keys.reshape(TOKENS, HEADS, HEAD_DIM)
    value_heads = values.reshape(TOKENS, HEADS, HEAD_DIM)
    segments = TOKENS // SEGMENT
    first = lax.map(one_segment, (query_heads.reshape(segments, SEGMENT, HEADS, HEAD_DIM),
                                  key_heads.reshape(segments, SEGMENT, HEADS, HEAD_DIM),
                                  value_heads.reshape(segments, SEGMENT, HEADS, HEAD_DIM)))
    state = (first[0].transpose(1, 0, 2).reshape(HEADS, TOKENS),
             first[1].transpose(1, 0, 2).reshape(HEADS, TOKENS),
             first[2].transpose(1, 0, 2, 3).reshape(HEADS, TOKENS, HEAD_DIM))
    far_level = attend_heads(select(query_heads, R3), select(key_heads, R3), select(value_heads, R3))
    state = merge_into(state, far_level, R3)
    result = state[2] / state[1][..., None]
    return result.transpose(1, 0, 2).reshape(TOKENS, WIDTH).astype(jnp.bfloat16)
```

```python
import functools

import jax
import jax.numpy as jnp
from jax import lax
from jax.experimental import pallas as pl
from jax.experimental.pallas import tpu as pltpu
from jax.sharding import Mesh
from jax.sharding import PartitionSpec as P

HEADS = 12
HEAD_DIM = 64
R3 = 128
OWN = 3
SPAN = OWN * HEAD_DIM
AXES = ("zl", "x", "y", "zh", "core")
SIZES = (8, 4, 4, 2, 2)
FACTOR = HEAD_DIM ** (-0.5) * 1.4426950408889634
BLANK = -1e30
F32 = jnp.float32
BF16 = jnp.bfloat16

KV = 768
QROWS = 384
PIECE = 1168


def route(dx=0, dy=0, dz=0, flip=0, by_core=False):
    pairs = []
    for src in range(512):
        rest, core = divmod(src, 2)
        rest, zh = divmod(rest, 2)
        rest, y = divmod(rest, 4)
        zl, x = divmod(rest, 4)
        sign = -1 if by_core and core else 1
        z = (zh * 8 + zl + sign * dz) % 16
        dst = ((((z % 8) * 4 + (x + dx) % 4) * 4 + (y + dy) % 4) * 2 + z // 8) * 2 + (core ^ flip)
        pairs.append((src, dst))
    return pairs


def move(array, **step):
    return lax.ppermute(array, AXES, route(**step))


def hop(array):
    return move(array, dz=4, by_core=True)


SMEM = pl.BlockSpec(memory_space=pltpu.SMEM)


def shape(*dims, dtype=BF16):
    return jax.ShapeDtypeStruct(dims, dtype)


def whole(*dims):
    return pl.BlockSpec(dims, lambda i: (0,) * len(dims))


def params():
    return pltpu.CompilerParams(vmem_limit_bytes=48 * 2**20)


def prep_kernel(
    y_ref, q_hbm, k_hbm, v_hbm, own_kv, staged, q_ref, k_ref, v_ref, sems
):
    copies = [
        pltpu.make_async_copy(source, target, sems.at[i])
        for i, (source, target) in enumerate(((k_hbm, k_ref), (v_hbm, v_ref), (q_hbm, q_ref)))
    ]
    for copy in copies:
        copy.start()
    y = y_ref[0]
    for copy in copies:
        copy.wait()
    keys = k_ref[...]
    keys32 = keys.astype(F32)
    values = v_ref[...].astype(F32)
    values_t = values.T.astype(BF16)
    queries_t = q_ref[...].astype(F32).T.astype(BF16)
    row = lax.broadcasted_iota(jnp.int32, (16, 768), 0)
    chosen = row == lax.broadcasted_iota(jnp.int32, (16, 768), 1) // HEAD_DIM
    picked = [
        jnp.sum(jnp.where(chosen, source[j * R3 : j * R3 + 16], 0.0), axis=0, keepdims=True)
        for source in (keys32, values)
        for j in range(2)
    ]
    for group in range(4):
        lo = group * SPAN
        part = keys32[:, lo : lo + SPAN]
        staged[group, 0:256, :] = part[:, 0:128].astype(BF16)
        staged[group, 256:384, :] = jnp.concatenate(
            [part[0:128, 128:192], part[128:256, 128:192]], axis=1
        ).astype(BF16)
        staged[group, 384:576, :] = values_t[lo : lo + SPAN, 0:128]
        staged[group, 576:768, :] = values_t[lo : lo + SPAN, 128:256]
        staged[group, 768:960, :] = queries_t[lo : lo + SPAN, 0:128]
        staged[group, 960:1152, :] = queries_t[lo : lo + SPAN, 128:256]
        far_rows = []
        for first, second in (picked[0:2], picked[2:4]):
            first, second = first[:, lo : lo + SPAN], second[:, lo : lo + SPAN]
            far_rows += [
                first[:, 0:128],
                second[:, 0:128],
                jnp.concatenate([first[:, 128:192], second[:, 128:192]], axis=1),
            ]
        far_rows.append(jnp.zeros((10, 128), F32))
        staged[group, 1152:1168, :] = jnp.concatenate(far_rows, axis=0).astype(BF16)
    own_kv[...] = staged[y, 0:KV, :]


def prep(y, queries, keys, values):
    return pl.pallas_call(
        prep_kernel,
        grid=(1,),
        out_shape=[shape(KV, 128), shape(4, PIECE, 128)],
        in_specs=[SMEM] + [pl.BlockSpec(memory_space=pltpu.HBM)] * 3,
        out_specs=[whole(KV, 128), whole(4, PIECE, 128)],
        scratch_shapes=[pltpu.VMEM((256, 768), BF16)] * 3 + [pltpu.SemaphoreType.DMA((3,))],
        compiler_params=params(),
        name="prep",
    )(y, queries, keys, values)


def sort_kernel(y_ref, got, all_kv, away_kv, q_out, far_out):
    y = y_ref[0]
    far_rows = []
    for i in range(4):
        all_kv[i * KV : (i + 1) * KV, :] = got[i, 0:KV, :]
        if i:
            away_kv[(i - 1) * KV : i * KV, :] = got[lax.rem(y + i, 4), 0:KV, :]
        q_out[i] = jnp.concatenate(
            [got[i, KV : KV + SPAN, :], got[i, KV + SPAN : KV + QROWS, :]], axis=1
        )
        far_rows.append(got[i, KV + QROWS : PIECE, :].astype(F32))
    blank = jnp.zeros((4, 128), F32)
    packed = []
    for base in (0, 3):
        packed += [rows[base : base + 2] for rows in far_rows]
        packed += [rows[base + 2 : base + 3] for rows in far_rows]
        packed.append(blank)
    packed = jnp.concatenate(packed, axis=0).astype(BF16)
    for i in range(16):
        far_out[i] = packed


def sort(y, got):
    shapes = [(4 * KV, 128), (3 * KV, 128), (4, SPAN, 256), (16, 32, 128)]
    return pl.pallas_call(
        sort_kernel,
        grid=(1,),
        out_shape=[shape(*dims) for dims in shapes],
        in_specs=[SMEM, whole(4, PIECE, 128)],
        out_specs=[whole(*dims) for dims in shapes],
        compiler_params=params(),
        name="sort",
    )(y, got)


def attend(blocks, queries, head, scores, first_peak):
    mine = queries[head * HEAD_DIM : (head + 1) * HEAD_DIM]
    blank = jnp.zeros_like(mine)
    low = jnp.concatenate([mine, blank], axis=0)
    high = jnp.concatenate([blank, mine], axis=0)
    top = None
    for i, (ref, base) in enumerate(blocks):
        if head < 2:
            parts = [(ref[base : base + 256, :], high if head else low)]
        else:
            third = ref[base + 256 : base + 384, :]
            parts = [(third, low), (third, high)]
        at = i * 256
        for rows, side in parts:
            s = jnp.dot(rows, side, preferred_element_type=F32)
            count = s.shape[0]
            scores[at : at + count, :] = s
            at += count
            here = jnp.max(s.reshape(count // 8, 8, 512), axis=0)
            top = here if top is None else jnp.maximum(top, here)
    peak = jnp.max(top, axis=0, keepdims=True)
    if first_peak is not None:
        peak = jnp.maximum(peak, first_peak)
    total = jnp.zeros((8, 512), F32)
    partial_value = jnp.zeros((HEAD_DIM, 512), F32)
    lo = head * HEAD_DIM
    for i, (ref, base) in enumerate(blocks):
        expos = jnp.exp2((scores[i * 256 : (i + 1) * 256, :] - peak) * FACTOR)
        total = total + jnp.sum(expos.reshape(32, 8, 512), axis=0)
        values = jnp.concatenate(
            [
                ref[base + 384 + lo : base + 384 + lo + HEAD_DIM, :],
                ref[base + 576 + lo : base + 576 + lo + HEAD_DIM, :],
            ],
            axis=1,
        )
        partial_value = partial_value + jnp.dot(
            values, expos.astype(BF16), preferred_element_type=F32
        )
    return peak, jnp.sum(total, axis=0, keepdims=True), partial_value


def near_kernel(counts, has_state, is_last, q_ref, *refs):
    refs = list(refs)
    blocks = []
    for count in counts:
        ref = refs.pop(0)
        blocks += [(ref, i * KV) for i in range(count)]
    if has_state:
        old_sum, old_stat = refs.pop(0), refs.pop(0)
    if is_last:
        far_sum, far_stat = refs.pop(0), refs.pop(0)
        out, scores = refs
    else:
        sum_out, stat_out, scores = refs
    queries = jnp.concatenate([q_ref[0], q_ref[1]], axis=1)
    peaks, totals = [], []
    for head in range(OWN):
        rows = slice(head * HEAD_DIM, (head + 1) * HEAD_DIM)
        first_peak = None
        if has_state:
            old_peak = old_stat[head : head + 1, :]
            old_total = old_stat[4 + head : 5 + head, :]
            first_peak = old_peak
        if is_last:
            far_peak = far_stat[head : head + 1, :]
            far_total = far_stat[8 + head : 9 + head, :]
            first_peak = jnp.maximum(old_peak, far_peak)
        peak, total, partial_value = attend(blocks, queries, head, scores.at[head], first_peak)
        if has_state:
            scale = jnp.exp2((old_peak - peak) * FACTOR)
            total = total + old_total * scale
            partial_value = partial_value + old_sum[rows, :] * scale
        if is_last:
            scale = jnp.exp2((far_peak - peak) * FACTOR)
            total = total + far_total * scale
            partial_value = partial_value + far_sum[rows, :] * scale
            result = (partial_value / total).astype(BF16)
            out[0, rows, :] = result[:, 0:256]
            out[1, rows, :] = result[:, 256:512]
        else:
            sum_out[rows, :] = partial_value
            peaks.append(peak)
            totals.append(total)
    if not is_last:
        blank = [jnp.zeros((1, 512), F32)]
        stat_out[...] = jnp.concatenate(peaks + blank + totals + blank, axis=0)


def near(queries, arrays, state=None, far_state=None):
    def along(rows):
        return pl.BlockSpec((rows, 512), lambda i: (0, i))

    counts = tuple(a.shape[0] // KV for a in arrays)
    is_last = far_state is not None
    two = pl.BlockSpec((2, SPAN, 256), lambda i: (i, 0, 0))
    operands = [queries, *arrays]
    in_specs = [two] + [whole(*a.shape) for a in arrays]
    if state is not None:
        operands += state
        in_specs += [along(SPAN), along(8)]
    if is_last:
        operands += far_state
        in_specs += [along(SPAN), along(16)]
        out_shape, out_specs = shape(4, SPAN, 256), two
    else:
        out_shape = [shape(SPAN, 1024, dtype=F32), shape(8, 1024, dtype=F32)]
        out_specs = [along(SPAN), along(8)]
    return pl.pallas_call(
        functools.partial(near_kernel, counts, state is not None, is_last),
        grid=(2,),
        out_shape=out_shape,
        in_specs=in_specs,
        out_specs=out_specs,
        scratch_shapes=[pltpu.VMEM((OWN, sum(counts) * 256, 512), F32)],
        compiler_params=params(),
        name="last" if is_last else "near",
    )(*operands)


def far_kernel(y_ref, q_ref, rows_ref, sum_out, stat_out):
    y = y_ref[0]
    place_r = lax.broadcasted_iota(jnp.int32, (1024, 128), 1)
    place = ((place_r // 2) % 4) * 256 + (place_r % 2) * 128 + y * OWN + place_r // 8
    lane = lax.broadcasted_iota(jnp.int32, (1024, 128), 0)
    pick = jnp.where((place_r < 24) & (lane == place), 1.0, 0.0)
    chosen = jnp.zeros((SPAN, 128), F32)
    for t in range(4):
        chosen = chosen + jnp.dot(
            q_ref[t], pick[t * 256 : (t + 1) * 256].astype(BF16), preferred_element_type=F32
        )
    row_head = lax.broadcasted_iota(jnp.int32, (SPAN, 128), 0) // HEAD_DIM
    r_head = lax.broadcasted_iota(jnp.int32, (SPAN, 128), 1) // 8
    mine = row_head == r_head
    chosen = jnp.where(mine, chosen, 0.0).astype(BF16)
    third = chosen[128:192]
    blank = jnp.zeros_like(third)

    gathered = rows_ref[...].astype(F32).reshape(128, 4, 8, 128)

    def section(i):
        return gathered[:, i].reshape(1024, 128)

    keys_a, keys_b = section(0).astype(BF16), section(1).astype(BF16)
    values_a = section(2).T.astype(BF16)
    values_b = section(3).T.astype(BF16)
    r = lax.broadcasted_iota(jnp.int32, (1024, 128), 1)
    key_row = lax.broadcasted_iota(jnp.int32, (1024, 128), 0)
    there_a = r < 16
    there_b = (r >= 16) & (key_row % 8 < 4)
    scores = [
        jnp.where(there, jnp.dot(rows, side, preferred_element_type=F32), BLANK)
        for rows, side, there in (
            (keys_a, chosen[0:128], there_a),
            (keys_b, jnp.concatenate([third, blank], axis=0), there_b),
            (keys_b, jnp.concatenate([blank, third], axis=0), there_b),
        )
    ]
    peak = functools.reduce(
        jnp.maximum, [jnp.max(s, axis=0, keepdims=True) for s in scores]
    )
    total = jnp.zeros((1, 128), F32)
    sums = []
    for s, values, there in zip(
        scores,
        (values_a, values_b[0:64], values_b[64:128]),
        (there_a, there_b, there_b),
    ):
        expos = jnp.where(there, jnp.exp2((s - peak) * FACTOR), 0.0)
        total = total + jnp.sum(expos, axis=0, keepdims=True)
        sums.append(jnp.dot(values, expos.astype(BF16), preferred_element_type=F32))
    partial_value = jnp.concatenate([sums[0], sums[1] + sums[2]], axis=0)
    partial_value = jnp.where(mine, partial_value, 0.0)
    head = lax.broadcasted_iota(jnp.int32, (8, 128), 0)
    r8 = lax.broadcasted_iota(jnp.int32, (8, 128), 1)
    same = (r8 // 8 == head) & (r8 < 24)
    wide = jnp.concatenate(
        [
            partial_value,
            jnp.where(same, peak, 0.0),
            jnp.where(same, total, 0.0),
            jnp.where(same, 1.0, 0.0),
        ],
        axis=0,
    )
    dense = lax.dot_general(
        wide,
        pick,
        (((1,), (1,)), ((), ())),
        precision=lax.Precision.HIGHEST,
        preferred_element_type=F32,
    )
    sum_out[...] = dense[0:SPAN]
    there = dense[SPAN + 16 : SPAN + 24] > 0.5
    stat_out[0:8, :] = jnp.where(there, dense[SPAN : SPAN + 8], BLANK)
    stat_out[8:16, :] = dense[SPAN + 8 : SPAN + 16]


def far(y, queries, rows):
    return pl.pallas_call(
        far_kernel,
        grid=(1,),
        out_shape=[shape(SPAN, 1024, dtype=F32), shape(16, 1024, dtype=F32)],
        in_specs=[SMEM, whole(4, SPAN, 256), whole(4096, 128)],
        out_specs=[whole(SPAN, 1024), whole(16, 1024)],
        compiler_params=params(),
        name="far",
    )(y, queries, rows)


def turn_kernel(in_ref, out_ref):
    out_ref[...] = in_ref[...].astype(F32).T.astype(BF16)


def turn(array):
    return pl.pallas_call(
        turn_kernel,
        grid=(1,),
        out_shape=shape(256, 768),
        in_specs=[whole(768, 256)],
        out_specs=whole(256, 768),
        compiler_params=params(),
        name="turn",
    )(array)


def body(queries, keys, values):
    y = lax.axis_index("y").astype(jnp.int32).reshape(1)
    own_kv, staged = prep(y, queries, keys, values)

    crossed_own = move(own_kv, dz=8)
    got = lax.all_to_all(staged, "y", 0, 0, tiled=True)
    crossed_own, got = lax.optimization_barrier((crossed_own, got))
    all_kv, away_kv, q, far_rows = sort(y, got)
    crossed_away = move(away_kv, dz=8)
    partner_kv = move(all_kv, flip=1)
    partner_own = move(crossed_own, flip=1)
    state = near(q, [all_kv])
    far_rows = lax.all_to_all(far_rows, ("zl", "zh"), 0, 0, tiled=True).reshape(512, 128)
    state, far_rows, partner_kv, partner_own = lax.optimization_barrier((state, far_rows, partner_kv, partner_own))
    state = near(q, [partner_kv], state)
    far_rows, *state = lax.optimization_barrier((far_rows, *state))
    far_rows = lax.all_to_all(
        jnp.broadcast_to(far_rows, (8, 512, 128)), ("x", "core"), 0, 0, tiled=True
    ).reshape(4096, 128)
    state, far_rows = lax.optimization_barrier((state, far_rows))
    state = near(q, [crossed_own, partner_own], state)
    far_state = far(y, q, far_rows)
    crossed_away, state, far_state = lax.optimization_barrier((crossed_away, state, far_state))
    partner_away = move(crossed_away, flip=1)
    state = near(q, [crossed_away], state)
    result = near(q, [partner_away], state, far_state)
    back = lax.all_to_all(result, "y", 0, 0, tiled=True)
    return turn(back.reshape(HEADS * HEAD_DIM, 256))


def solution(mesh):
    fine = Mesh(mesh.devices.reshape(SIZES), AXES)
    placed = P(AXES, None)
    return jax.shard_map(
        body, mesh=fine, in_specs=(placed,) * 3, out_specs=placed, check_vma=False
    )
```

```python
import functools

import jax
import jax.numpy as jnp
from jax import lax
from jax.experimental import pallas as pl
from jax.experimental.pallas import tpu as pltpu
from jax.sharding import Mesh
from jax.sharding import PartitionSpec as P

HEADS = 12
HEAD_DIM = 64
R3 = 128
OWN = 3
SPAN = OWN * HEAD_DIM
AXES = ("zl", "x", "y", "zh", "core")
SIZES = (8, 4, 4, 2, 2)
FACTOR = HEAD_DIM ** (-0.5) * 1.4426950408889634
BLANK = -1e30
F32 = jnp.float32
BF16 = jnp.bfloat16

KV = 768
QROWS = 384
PIECE = 1152


def route(dx=0, dy=0, dz=0, flip=0, by_core=False):
    pairs = []
    for src in range(512):
        rest, core = divmod(src, 2)
        rest, zh = divmod(rest, 2)
        rest, y = divmod(rest, 4)
        zl, x = divmod(rest, 4)
        sign = -1 if by_core and core else 1
        z = (zh * 8 + zl + sign * dz) % 16
        dst = ((((z % 8) * 4 + (x + dx) % 4) * 4 + (y + dy) % 4) * 2 + z // 8) * 2 + (core ^ flip)
        pairs.append((src, dst))
    return pairs


def move(array, **step):
    return lax.ppermute(array, AXES, route(**step))


def hop(array):
    return move(array, dz=4, by_core=True)


SMEM = pl.BlockSpec(memory_space=pltpu.SMEM)


def shape(*dims, dtype=BF16):
    return jax.ShapeDtypeStruct(dims, dtype)


def whole(*dims):
    return pl.BlockSpec(dims, lambda i: (0,) * len(dims))


FREE = pl.CostEstimate(flops=1, transcendentals=0, bytes_accessed=1)


def params():
    return pltpu.CompilerParams(vmem_limit_bytes=48 * 2**20)


def prep_kernel(
    q_hbm, k_hbm, v_hbm, staged, far_out, q_ref, k_ref, v_ref, sems
):
    copies = [
        pltpu.make_async_copy(source, target, sems.at[i])
        for i, (source, target) in enumerate(((k_hbm, k_ref), (v_hbm, v_ref), (q_hbm, q_ref)))
    ]
    for copy in copies:
        copy.start()
    for copy in copies:
        copy.wait()
    keys = k_ref[...]
    keys32 = keys.astype(F32)
    values = v_ref[...].astype(F32)
    values_t = values.T.astype(BF16)
    queries_t = q_ref[...].astype(F32).T.astype(BF16)
    row = lax.broadcasted_iota(jnp.int32, (16, 768), 0)
    chosen = row == lax.broadcasted_iota(jnp.int32, (16, 768), 1) // HEAD_DIM
    picked = [
        jnp.sum(jnp.where(chosen, source[j * R3 : j * R3 + 16], 0.0), axis=0, keepdims=True)
        for source in (keys32, values)
        for j in range(2)
    ]
    packed = []
    for group in range(4):
        lo = group * SPAN
        part = keys32[:, lo : lo + SPAN]
        staged[group, 0:256, :] = part[:, 0:128].astype(BF16)
        staged[group, 256:384, :] = jnp.concatenate(
            [part[0:128, 128:192], part[128:256, 128:192]], axis=1
        ).astype(BF16)
        staged[group, 384:576, :] = values_t[lo : lo + SPAN, 0:128]
        staged[group, 576:768, :] = values_t[lo : lo + SPAN, 128:256]
        staged[group, 768:960, :] = queries_t[lo : lo + SPAN, 0:128]
        staged[group, 960:1152, :] = queries_t[lo : lo + SPAN, 128:256]
        far_rows = []
        for first, second in (picked[0:2], picked[2:4]):
            first, second = first[:, lo : lo + SPAN], second[:, lo : lo + SPAN]
            far_rows += [
                first[:, 0:128],
                second[:, 0:128],
                jnp.concatenate([first[:, 128:192], second[:, 128:192]], axis=1),
            ]
        packed += far_rows + [jnp.zeros((2, 128), F32)]
    packed = jnp.concatenate(packed, axis=0).astype(BF16)
    for i in range(16):
        far_out[i] = packed


def prep(queries, keys, values):
    return pl.pallas_call(
        prep_kernel,
        grid=(1,),
        out_shape=[shape(4, PIECE, 128), shape(16, 32, 128)],
        in_specs=[pl.BlockSpec(memory_space=pltpu.HBM)] * 3,
        out_specs=[whole(4, PIECE, 128), whole(16, 32, 128)],
        scratch_shapes=[pltpu.VMEM((256, 768), BF16)] * 3 + [pltpu.SemaphoreType.DMA((3,))],
        compiler_params=params(),
        name="prep",
    )(queries, keys, values)


def sort_kernel(got, all_kv, q_out):
    for i in range(4):
        all_kv[i * KV : (i + 1) * KV, :] = got[i, 0:KV, :]
        q_out[i] = jnp.concatenate(
            [got[i, KV : KV + SPAN, :], got[i, KV + SPAN : PIECE, :]], axis=1
        )


def sort(got):
    shapes = [(4 * KV, 128), (4, SPAN, 256)]
    return pl.pallas_call(
        sort_kernel,
        grid=(1,),
        out_shape=[shape(*dims) for dims in shapes],
        in_specs=[whole(4, PIECE, 128)],
        out_specs=[whole(*dims) for dims in shapes],
        compiler_params=params(),
        cost_estimate=FREE,
        name="sort",
    )(got)


def spread_kernel(rows_ref, out):
    rows = rows_ref[...].astype(F32).reshape(16, 4, 8, 128)
    for group in range(4):
        part = rows[:, group]
        kinds = []
        for base in (0, 3):
            kinds += [part[i, base : base + 2] for i in range(16)]
            kinds += [part[i, base + 2 : base + 3] for i in range(16)]
        packed = jnp.concatenate(kinds, axis=0).astype(BF16)
        for x in range(4):
            for core in range(2):
                out[(x * 4 + group) * 2 + core] = packed


def spread(rows):
    return pl.pallas_call(
        spread_kernel,
        grid=(1,),
        out_shape=shape(32, 96, 128),
        in_specs=[whole(16, 32, 128)],
        out_specs=whole(32, 96, 128),
        compiler_params=params(),
        cost_estimate=FREE,
        name="spread",
    )(rows)


def attend(blocks, queries, head, scores, first_peak):
    mine = queries[head * HEAD_DIM : (head + 1) * HEAD_DIM]
    blank = jnp.zeros_like(mine)
    low = jnp.concatenate([mine, blank], axis=0)
    high = jnp.concatenate([blank, mine], axis=0)
    top = None
    for i, (ref, base) in enumerate(blocks):
        if head < 2:
            parts = [(ref[base : base + 256, :], high if head else low)]
        else:
            third = ref[base + 256 : base + 384, :]
            parts = [(third, low), (third, high)]
        at = i * 256
        for rows, side in parts:
            s = jnp.dot(rows, side, preferred_element_type=F32)
            count = s.shape[0]
            scores[at : at + count, :] = s
            at += count
            here = jnp.max(s.reshape(count // 8, 8, 512), axis=0)
            top = here if top is None else jnp.maximum(top, here)
    peak = jnp.max(top, axis=0, keepdims=True)
    if first_peak is not None:
        peak = jnp.maximum(peak, first_peak)
    total = jnp.zeros((8, 512), F32)
    partial_value = jnp.zeros((HEAD_DIM, 512), F32)
    lo = head * HEAD_DIM
    for i, (ref, base) in enumerate(blocks):
        expos = jnp.exp2((scores[i * 256 : (i + 1) * 256, :] - peak) * FACTOR)
        total = total + jnp.sum(expos.reshape(32, 8, 512), axis=0)
        values = jnp.concatenate(
            [
                ref[base + 384 + lo : base + 384 + lo + HEAD_DIM, :],
                ref[base + 576 + lo : base + 576 + lo + HEAD_DIM, :],
            ],
            axis=1,
        )
        partial_value = partial_value + jnp.dot(
            values, expos.astype(BF16), preferred_element_type=F32
        )
    return peak, jnp.sum(total, axis=0, keepdims=True), partial_value


def near_kernel(counts, has_state, is_last, q_ref, *refs):
    refs = list(refs)
    blocks = []
    for count in counts:
        ref = refs.pop(0)
        blocks += [(ref, i * KV) for i in range(count)]
    if has_state:
        old_sum, old_stat = refs.pop(0), refs.pop(0)
    if is_last:
        far_sum, far_stat = refs.pop(0), refs.pop(0)
        out, scores = refs
    else:
        sum_out, stat_out, scores = refs
    queries = jnp.concatenate([q_ref[0], q_ref[1]], axis=1)
    peaks, totals = [], []
    for head in range(OWN):
        rows = slice(head * HEAD_DIM, (head + 1) * HEAD_DIM)
        first_peak = None
        if has_state:
            old_peak = old_stat[head : head + 1, :]
            old_total = old_stat[4 + head : 5 + head, :]
            first_peak = old_peak
        if is_last:
            far_peak = far_stat[head : head + 1, :]
            far_total = far_stat[8 + head : 9 + head, :]
            first_peak = jnp.maximum(old_peak, far_peak)
        peak, total, partial_value = attend(blocks, queries, head, scores.at[head], first_peak)
        if has_state:
            scale = jnp.exp2((old_peak - peak) * FACTOR)
            total = total + old_total * scale
            partial_value = partial_value + old_sum[rows, :] * scale
        if is_last:
            scale = jnp.exp2((far_peak - peak) * FACTOR)
            total = total + far_total * scale
            partial_value = partial_value + far_sum[rows, :] * scale
            result = (partial_value / total).astype(BF16)
            out[0, rows, :] = result[:, 0:256]
            out[1, rows, :] = result[:, 256:512]
        else:
            sum_out[rows, :] = partial_value
            peaks.append(peak)
            totals.append(total)
    if not is_last:
        blank = [jnp.zeros((1, 512), F32)]
        stat_out[...] = jnp.concatenate(peaks + blank + totals + blank, axis=0)


def near(queries, arrays, state=None, far_state=None):
    def along(rows):
        return pl.BlockSpec((rows, 512), lambda i: (0, i))

    counts = tuple(a.shape[0] // KV for a in arrays)
    is_last = far_state is not None
    two = pl.BlockSpec((2, SPAN, 256), lambda i: (i, 0, 0))
    operands = [queries, *arrays]
    in_specs = [two] + [whole(*a.shape) for a in arrays]
    if state is not None:
        operands += state
        in_specs += [along(SPAN), along(8)]
    if is_last:
        operands += far_state
        in_specs += [along(SPAN), along(16)]
        out_shape, out_specs = shape(4, SPAN, 256), two
    else:
        out_shape = [shape(SPAN, 1024, dtype=F32), shape(8, 1024, dtype=F32)]
        out_specs = [along(SPAN), along(8)]
    return pl.pallas_call(
        functools.partial(near_kernel, counts, state is not None, is_last),
        grid=(2,),
        out_shape=out_shape,
        in_specs=in_specs,
        out_specs=out_specs,
        scratch_shapes=[pltpu.VMEM((OWN, sum(counts) * 256, 512), F32)],
        compiler_params=params(),
        name="last" if is_last else "near",
    )(*operands)


def far_kernel(y_ref, q_ref, rows_ref, sum_out, stat_out):
    y = y_ref[0]
    place_r = lax.broadcasted_iota(jnp.int32, (1024, 128), 1)
    place = ((place_r // 2) % 4) * 256 + (place_r % 2) * 128 + y * OWN + place_r // 8
    lane = lax.broadcasted_iota(jnp.int32, (1024, 128), 0)
    pick = jnp.where((place_r < 24) & (lane == place), 1.0, 0.0)
    chosen = jnp.zeros((SPAN, 128), F32)
    for t in range(4):
        chosen = chosen + jnp.dot(
            q_ref[t], pick[t * 256 : (t + 1) * 256].astype(BF16), preferred_element_type=F32
        )
    row_head = lax.broadcasted_iota(jnp.int32, (SPAN, 128), 0) // HEAD_DIM
    r_head = lax.broadcasted_iota(jnp.int32, (SPAN, 128), 1) // 8
    mine = row_head == r_head
    chosen = jnp.where(mine, chosen, 0.0).astype(BF16)
    third = chosen[128:192]
    blank = jnp.zeros_like(third)

    def section(low, high):
        return rows_ref[:, low:high, :].reshape(32 * (high - low), 128)

    keys_a, keys_b = section(0, 32), section(32, 48)
    values_a = section(48, 80).astype(F32).T.astype(BF16)
    values_b = section(80, 96).astype(F32).T.astype(BF16)
    r = lax.broadcasted_iota(jnp.int32, (1, 128), 1)
    there_a, there_b = r < 16, r >= 16
    scores = [
        jnp.where(there, jnp.dot(rows, side, preferred_element_type=F32), BLANK)
        for rows, side, there in (
            (keys_a, chosen[0:128], there_a),
            (keys_b, jnp.concatenate([third, blank], axis=0), there_b),
            (keys_b, jnp.concatenate([blank, third], axis=0), there_b),
        )
    ]
    peak = functools.reduce(
        jnp.maximum, [jnp.max(s, axis=0, keepdims=True) for s in scores]
    )
    total = jnp.zeros((1, 128), F32)
    sums = []
    for s, values, there in zip(
        scores,
        (values_a, values_b[0:64], values_b[64:128]),
        (there_a, there_b, there_b),
    ):
        expos = jnp.where(there, jnp.exp2((s - peak) * FACTOR), 0.0)
        total = total + jnp.sum(expos, axis=0, keepdims=True)
        sums.append(jnp.dot(values, expos.astype(BF16), preferred_element_type=F32))
    partial_value = jnp.concatenate([sums[0], sums[1] + sums[2]], axis=0)
    partial_value = jnp.where(mine, partial_value, 0.0)
    head = lax.broadcasted_iota(jnp.int32, (8, 128), 0)
    r8 = lax.broadcasted_iota(jnp.int32, (8, 128), 1)
    same = (r8 // 8 == head) & (r8 < 24)
    wide = jnp.concatenate(
        [
            partial_value,
            jnp.where(same, peak, 0.0),
            jnp.where(same, total, 0.0),
            jnp.where(same, 1.0, 0.0),
        ],
        axis=0,
    )
    dense = lax.dot_general(
        wide,
        pick,
        (((1,), (1,)), ((), ())),
        precision=lax.Precision.HIGHEST,
        preferred_element_type=F32,
    )
    sum_out[...] = dense[0:SPAN]
    there = dense[SPAN + 16 : SPAN + 24] > 0.5
    stat_out[0:8, :] = jnp.where(there, dense[SPAN : SPAN + 8], BLANK)
    stat_out[8:16, :] = dense[SPAN + 8 : SPAN + 16]


def far(y, queries, rows):
    return pl.pallas_call(
        far_kernel,
        grid=(1,),
        out_shape=[shape(SPAN, 1024, dtype=F32), shape(16, 1024, dtype=F32)],
        in_specs=[SMEM, whole(4, SPAN, 256), whole(32, 96, 128)],
        out_specs=[whole(SPAN, 1024), whole(16, 1024)],
        compiler_params=params(),
        name="far",
    )(y, queries, rows)


def turn_kernel(in_ref, out_ref):
    out_ref[...] = in_ref[...].astype(F32).T.astype(BF16)


def turn(array):
    return pl.pallas_call(
        turn_kernel,
        grid=(1,),
        out_shape=shape(256, 768),
        in_specs=[whole(768, 256)],
        out_specs=whole(256, 768),
        compiler_params=params(),
        name="turn",
    )(array)


def body(queries, keys, values):
    y = lax.axis_index("y").astype(jnp.int32).reshape(1)
    staged, far_rows = prep(queries, keys, values)
    got = lax.all_to_all(staged, "y", 0, 0, tiled=True)
    far_rows = spread(lax.all_to_all(far_rows, ("zl", "zh"), 0, 0, tiled=True))
    far_rows = lax.all_to_all(far_rows, ("x", "y", "core"), 0, 0, tiled=True)
    all_kv, q = sort(got)
    crossed = move(all_kv, dz=8)
    partner_kv = move(all_kv, flip=1)
    all_kv, partner_kv, far_rows = lax.optimization_barrier((all_kv, partner_kv, far_rows))
    far_state = far(y, q, far_rows)
    state = near(q, [all_kv, partner_kv])
    crossed, state, far_state = lax.optimization_barrier((crossed, state, far_state))
    partner_crossed = move(crossed, flip=1)
    state = near(q, [crossed], state)
    result = near(q, [partner_crossed], state, far_state)
    back = lax.all_to_all(result, "y", 0, 0, tiled=True)
    return turn(back.reshape(HEADS * HEAD_DIM, 256))


def solution(mesh):
    fine = Mesh(mesh.devices.reshape(SIZES), AXES)
    placed = P(AXES, None)
    return jax.shard_map(
        body, mesh=fine, in_specs=(placed,) * 3, out_specs=placed, check_vma=False
    )
```

```python
import functools

import jax
import jax.numpy as jnp
from jax import lax
from jax.experimental import pallas as pl
from jax.experimental.pallas import tpu as pltpu
from jax.sharding import Mesh
from jax.sharding import PartitionSpec as P

HEADS = 12
HEAD_DIM = 64
R3 = 128
OWN = 3
SPAN = OWN * HEAD_DIM
AXES = ("zl", "x", "y", "zh", "core")
SIZES = (8, 4, 4, 2, 2)
FACTOR = HEAD_DIM ** (-0.5) * 1.4426950408889634
BLANK = -1e30
F32 = jnp.float32
BF16 = jnp.bfloat16

KV = 768
QROWS = 384
PIECE = 1152


def route(dx=0, dy=0, dz=0, flip=0, by_core=False):
    pairs = []
    for src in range(512):
        rest, core = divmod(src, 2)
        rest, zh = divmod(rest, 2)
        rest, y = divmod(rest, 4)
        zl, x = divmod(rest, 4)
        sign = -1 if by_core and core else 1
        z = (zh * 8 + zl + sign * dz) % 16
        dst = ((((z % 8) * 4 + (x + dx) % 4) * 4 + (y + dy) % 4) * 2 + z // 8) * 2 + (core ^ flip)
        pairs.append((src, dst))
    return pairs


def move(array, **step):
    return lax.ppermute(array, AXES, route(**step))


def hop(array):
    return move(array, dz=4, by_core=True)


SMEM = pl.BlockSpec(memory_space=pltpu.SMEM)


def shape(*dims, dtype=BF16):
    return jax.ShapeDtypeStruct(dims, dtype)


def whole(*dims):
    return pl.BlockSpec(dims, lambda i: (0,) * len(dims))


FREE = pl.CostEstimate(flops=1, transcendentals=0, bytes_accessed=1)


def params():
    return pltpu.CompilerParams(vmem_limit_bytes=48 * 2**20)


def prep_kernel(
    y_ref, q_hbm, k_hbm, v_hbm, staged, far_out, cross_0, cross_1, cross_2, cross_3,
    q_ref, k_ref, v_ref, sems,
):
    copies = [
        pltpu.make_async_copy(source, target, sems.at[i])
        for i, (source, target) in enumerate(((k_hbm, k_ref), (v_hbm, v_ref), (q_hbm, q_ref)))
    ]
    for copy in copies:
        copy.start()
    for copy in copies:
        copy.wait()
    keys = k_ref[...]
    keys32 = keys.astype(F32)
    values = v_ref[...].astype(F32)
    values_t = values.T.astype(BF16)
    queries_t = q_ref[...].astype(F32).T.astype(BF16)
    row = lax.broadcasted_iota(jnp.int32, (16, 768), 0)
    chosen = row == lax.broadcasted_iota(jnp.int32, (16, 768), 1) // HEAD_DIM
    picked = [
        jnp.sum(jnp.where(chosen, source[j * R3 : j * R3 + 16], 0.0), axis=0, keepdims=True)
        for source in (keys32, values)
        for j in range(2)
    ]
    packed = []
    for group in range(4):
        lo = group * SPAN
        part = keys32[:, lo : lo + SPAN]
        staged[group, 0:256, :] = part[:, 0:128].astype(BF16)
        staged[group, 256:384, :] = jnp.concatenate(
            [part[0:128, 128:192], part[128:256, 128:192]], axis=1
        ).astype(BF16)
        staged[group, 384:576, :] = values_t[lo : lo + SPAN, 0:128]
        staged[group, 576:768, :] = values_t[lo : lo + SPAN, 128:256]
        staged[group, 768:960, :] = queries_t[lo : lo + SPAN, 0:128]
        staged[group, 960:1152, :] = queries_t[lo : lo + SPAN, 128:256]
        far_rows = []
        for first, second in (picked[0:2], picked[2:4]):
            first, second = first[:, lo : lo + SPAN], second[:, lo : lo + SPAN]
            far_rows += [
                first[:, 0:128],
                second[:, 0:128],
                jnp.concatenate([first[:, 128:192], second[:, 128:192]], axis=1),
            ]
        packed += far_rows + [jnp.zeros((2, 128), F32)]
    packed = jnp.concatenate(packed, axis=0).astype(BF16)
    for i in range(16):
        far_out[i] = packed
    for i, out in enumerate((cross_0, cross_1, cross_2, cross_3)):
        out[...] = staged[lax.rem(y_ref[0] + i, 4), 0:KV, :]


def prep(y, queries, keys, values):
    return pl.pallas_call(
        prep_kernel,
        grid=(1,),
        out_shape=[shape(4, PIECE, 128), shape(16, 32, 128)] + [shape(KV, 128)] * 4,
        in_specs=[SMEM] + [pl.BlockSpec(memory_space=pltpu.HBM)] * 3,
        out_specs=[whole(4, PIECE, 128), whole(16, 32, 128)] + [whole(KV, 128)] * 4,
        scratch_shapes=[pltpu.VMEM((256, 768), BF16)] * 3 + [pltpu.SemaphoreType.DMA((3,))],
        compiler_params=params(),
        name="prep",
    )(y, queries, keys, values)


def sort_kernel(got, all_kv, q_out):
    for i in range(4):
        all_kv[i * KV : (i + 1) * KV, :] = got[i, 0:KV, :]
        q_out[i] = jnp.concatenate(
            [got[i, KV : KV + SPAN, :], got[i, KV + SPAN : PIECE, :]], axis=1
        )


def sort(got):
    shapes = [(4 * KV, 128), (4, SPAN, 256)]
    return pl.pallas_call(
        sort_kernel,
        grid=(1,),
        out_shape=[shape(*dims) for dims in shapes],
        in_specs=[whole(4, PIECE, 128)],
        out_specs=[whole(*dims) for dims in shapes],
        compiler_params=params(),
        cost_estimate=FREE,
        name="sort",
    )(got)


def spread_kernel(rows_ref, out):
    rows = rows_ref[...].astype(F32).reshape(16, 4, 8, 128)
    for group in range(4):
        part = rows[:, group]
        kinds = []
        for base in (0, 3):
            kinds += [part[i, base : base + 2] for i in range(16)]
            kinds += [part[i, base + 2 : base + 3] for i in range(16)]
        packed = jnp.concatenate(kinds, axis=0).astype(BF16)
        for x in range(4):
            for core in range(2):
                out[(x * 4 + group) * 2 + core] = packed


def spread(rows):
    return pl.pallas_call(
        spread_kernel,
        grid=(1,),
        out_shape=shape(32, 96, 128),
        in_specs=[whole(16, 32, 128)],
        out_specs=whole(32, 96, 128),
        compiler_params=params(),
        cost_estimate=FREE,
        name="spread",
    )(rows)


def attend(blocks, queries, head, scores, first_peak):
    mine = queries[head * HEAD_DIM : (head + 1) * HEAD_DIM]
    blank = jnp.zeros_like(mine)
    low = jnp.concatenate([mine, blank], axis=0)
    high = jnp.concatenate([blank, mine], axis=0)
    top = None
    for i, (ref, base) in enumerate(blocks):
        if head < 2:
            parts = [(ref[base : base + 256, :], high if head else low)]
        else:
            third = ref[base + 256 : base + 384, :]
            parts = [(third, low), (third, high)]
        at = i * 256
        for rows, side in parts:
            s = jnp.dot(rows, side, preferred_element_type=F32)
            count = s.shape[0]
            scores[at : at + count, :] = s
            at += count
            here = jnp.max(s.reshape(count // 8, 8, 512), axis=0)
            top = here if top is None else jnp.maximum(top, here)
    peak = jnp.max(top, axis=0, keepdims=True)
    if first_peak is not None:
        peak = jnp.maximum(peak, first_peak)
    total = jnp.zeros((8, 512), F32)
    partial_value = jnp.zeros((HEAD_DIM, 512), F32)
    lo = head * HEAD_DIM
    for i, (ref, base) in enumerate(blocks):
        expos = jnp.exp2((scores[i * 256 : (i + 1) * 256, :] - peak) * FACTOR)
        total = total + jnp.sum(expos.reshape(32, 8, 512), axis=0)
        values = jnp.concatenate(
            [
                ref[base + 384 + lo : base + 384 + lo + HEAD_DIM, :],
                ref[base + 576 + lo : base + 576 + lo + HEAD_DIM, :],
            ],
            axis=1,
        )
        partial_value = partial_value + jnp.dot(
            values, expos.astype(BF16), preferred_element_type=F32
        )
    return peak, jnp.sum(total, axis=0, keepdims=True), partial_value


def near_kernel(counts, has_state, is_last, q_ref, *refs):
    refs = list(refs)
    blocks = []
    for count in counts:
        ref = refs.pop(0)
        blocks += [(ref, i * KV) for i in range(count)]
    if has_state:
        old_sum, old_stat = refs.pop(0), refs.pop(0)
    if is_last:
        far_sum, far_stat = refs.pop(0), refs.pop(0)
        out, scores = refs
    else:
        sum_out, stat_out, scores = refs
    queries = jnp.concatenate([q_ref[0], q_ref[1]], axis=1)
    peaks, totals = [], []
    for head in range(OWN):
        rows = slice(head * HEAD_DIM, (head + 1) * HEAD_DIM)
        first_peak = None
        if has_state:
            old_peak = old_stat[head : head + 1, :]
            old_total = old_stat[4 + head : 5 + head, :]
            first_peak = old_peak
        if is_last:
            far_peak = far_stat[head : head + 1, :]
            far_total = far_stat[8 + head : 9 + head, :]
            first_peak = jnp.maximum(old_peak, far_peak)
        peak, total, partial_value = attend(blocks, queries, head, scores.at[head], first_peak)
        if has_state:
            scale = jnp.exp2((old_peak - peak) * FACTOR)
            total = total + old_total * scale
            partial_value = partial_value + old_sum[rows, :] * scale
        if is_last:
            scale = jnp.exp2((far_peak - peak) * FACTOR)
            total = total + far_total * scale
            partial_value = partial_value + far_sum[rows, :] * scale
            result = (partial_value / total).astype(BF16)
            out[0, rows, :] = result[:, 0:256]
            out[1, rows, :] = result[:, 256:512]
        else:
            sum_out[rows, :] = partial_value
            peaks.append(peak)
            totals.append(total)
    if not is_last:
        blank = [jnp.zeros((1, 512), F32)]
        stat_out[...] = jnp.concatenate(peaks + blank + totals + blank, axis=0)


def near(queries, arrays, state=None, far_state=None):
    def along(rows):
        return pl.BlockSpec((rows, 512), lambda i: (0, i))

    counts = tuple(a.shape[0] // KV for a in arrays)
    is_last = far_state is not None
    two = pl.BlockSpec((2, SPAN, 256), lambda i: (i, 0, 0))
    operands = [queries, *arrays]
    in_specs = [two] + [whole(*a.shape) for a in arrays]
    if state is not None:
        operands += state
        in_specs += [along(SPAN), along(8)]
    if is_last:
        operands += far_state
        in_specs += [along(SPAN), along(16)]
        out_shape, out_specs = shape(4, SPAN, 256), two
    else:
        out_shape = [shape(SPAN, 1024, dtype=F32), shape(8, 1024, dtype=F32)]
        out_specs = [along(SPAN), along(8)]
    return pl.pallas_call(
        functools.partial(near_kernel, counts, state is not None, is_last),
        grid=(2,),
        out_shape=out_shape,
        in_specs=in_specs,
        out_specs=out_specs,
        scratch_shapes=[pltpu.VMEM((OWN, sum(counts) * 256, 512), F32)],
        compiler_params=params(),
        name="last" if is_last else "near",
    )(*operands)


def far_kernel(y_ref, q_ref, rows_ref, sum_out, stat_out):
    y = y_ref[0]
    place_r = lax.broadcasted_iota(jnp.int32, (1024, 128), 1)
    place = ((place_r // 2) % 4) * 256 + (place_r % 2) * 128 + y * OWN + place_r // 8
    lane = lax.broadcasted_iota(jnp.int32, (1024, 128), 0)
    pick = jnp.where((place_r < 24) & (lane == place), 1.0, 0.0)
    chosen = jnp.zeros((SPAN, 128), F32)
    for t in range(4):
        chosen = chosen + jnp.dot(
            q_ref[t], pick[t * 256 : (t + 1) * 256].astype(BF16), preferred_element_type=F32
        )
    row_head = lax.broadcasted_iota(jnp.int32, (SPAN, 128), 0) // HEAD_DIM
    r_head = lax.broadcasted_iota(jnp.int32, (SPAN, 128), 1) // 8
    mine = row_head == r_head
    chosen = jnp.where(mine, chosen, 0.0).astype(BF16)
    third = chosen[128:192]
    blank = jnp.zeros_like(third)

    def section(low, high):
        return rows_ref[:, low:high, :].reshape(32 * (high - low), 128)

    keys_a, keys_b = section(0, 32), section(32, 48)
    values_a = section(48, 80).astype(F32).T.astype(BF16)
    values_b = section(80, 96).astype(F32).T.astype(BF16)
    r = lax.broadcasted_iota(jnp.int32, (1, 128), 1)
    there_a, there_b = r < 16, r >= 16
    scores = [
        jnp.where(there, jnp.dot(rows, side, preferred_element_type=F32), BLANK)
        for rows, side, there in (
            (keys_a, chosen[0:128], there_a),
            (keys_b, jnp.concatenate([third, blank], axis=0), there_b),
            (keys_b, jnp.concatenate([blank, third], axis=0), there_b),
        )
    ]
    peak = functools.reduce(
        jnp.maximum, [jnp.max(s, axis=0, keepdims=True) for s in scores]
    )
    total = jnp.zeros((1, 128), F32)
    sums = []
    for s, values, there in zip(
        scores,
        (values_a, values_b[0:64], values_b[64:128]),
        (there_a, there_b, there_b),
    ):
        expos = jnp.where(there, jnp.exp2((s - peak) * FACTOR), 0.0)
        total = total + jnp.sum(expos, axis=0, keepdims=True)
        sums.append(jnp.dot(values, expos.astype(BF16), preferred_element_type=F32))
    partial_value = jnp.concatenate([sums[0], sums[1] + sums[2]], axis=0)
    partial_value = jnp.where(mine, partial_value, 0.0)
    head = lax.broadcasted_iota(jnp.int32, (8, 128), 0)
    r8 = lax.broadcasted_iota(jnp.int32, (8, 128), 1)
    same = (r8 // 8 == head) & (r8 < 24)
    wide = jnp.concatenate(
        [
            partial_value,
            jnp.where(same, peak, 0.0),
            jnp.where(same, total, 0.0),
            jnp.where(same, 1.0, 0.0),
        ],
        axis=0,
    )
    dense = lax.dot_general(
        wide,
        pick,
        (((1,), (1,)), ((), ())),
        precision=lax.Precision.HIGHEST,
        preferred_element_type=F32,
    )
    sum_out[...] = dense[0:SPAN]
    there = dense[SPAN + 16 : SPAN + 24] > 0.5
    stat_out[0:8, :] = jnp.where(there, dense[SPAN : SPAN + 8], BLANK)
    stat_out[8:16, :] = dense[SPAN + 8 : SPAN + 16]


def far(y, queries, rows):
    return pl.pallas_call(
        far_kernel,
        grid=(1,),
        out_shape=[shape(SPAN, 1024, dtype=F32), shape(16, 1024, dtype=F32)],
        in_specs=[SMEM, whole(4, SPAN, 256), whole(32, 96, 128)],
        out_specs=[whole(SPAN, 1024), whole(16, 1024)],
        compiler_params=params(),
        name="far",
    )(y, queries, rows)


def turn_kernel(in_ref, out_ref):
    out_ref[...] = in_ref[...].astype(F32).T.astype(BF16)


def turn(array):
    return pl.pallas_call(
        turn_kernel,
        grid=(1,),
        out_shape=shape(256, 768),
        in_specs=[whole(768, 256)],
        out_specs=whole(256, 768),
        compiler_params=params(),
        name="turn",
    )(array)


def own_half(y, staged, far_rows):
    got = lax.all_to_all(staged, "y", 0, 0, tiled=True)
    far_rows = spread(lax.all_to_all(far_rows, ("zl", "zh"), 0, 0, tiled=True))
    far_rows = lax.all_to_all(far_rows, ("x", "y", "core"), 0, 0, tiled=True)
    all_kv, q = sort(got)
    partner_kv = move(all_kv, flip=1)
    state = near(q, [all_kv, partner_kv])
    return q, tuple(state), tuple(far(y, q, far_rows))


def body(queries, keys, values):
    y = lax.axis_index("y").astype(jnp.int32).reshape(1)
    staged, far_rows, *cross = prep(y, queries, keys, values)
    crossed = [move(a, dy=i, dz=8) for i, a in enumerate(cross)]

    def blank(*args):
        return jax.tree.map(lambda a: jnp.zeros(a.shape, a.dtype), jax.eval_shape(own_half, *args))

    q, state, far_state = lax.cond(y[0] < 4, own_half, blank, y, staged, far_rows)
    crossed, state, far_state = lax.optimization_barrier((crossed, state, far_state))
    crossed = jnp.concatenate(crossed, axis=0)
    partner_crossed = move(crossed, flip=1)
    state = near(q, [crossed], state)
    result = near(q, [partner_crossed], state, far_state)
    back = lax.all_to_all(result, "y", 0, 0, tiled=True)
    return turn(back.reshape(HEADS * HEAD_DIM, 256))


def solution(mesh):
    fine = Mesh(mesh.devices.reshape(SIZES), AXES)
    placed = P(AXES, None)
    return jax.shard_map(
        body, mesh=fine, in_specs=(placed,) * 3, out_specs=placed, check_vma=False
    )
```

```python
import functools

import jax
import jax.numpy as jnp
from jax import lax
from jax.experimental import pallas as pl
from jax.experimental.pallas import tpu as pltpu
from jax.sharding import Mesh
from jax.sharding import PartitionSpec as P

HEADS = 12
HEAD_DIM = 64
R3 = 128
OWN = 3
SPAN = OWN * HEAD_DIM
AXES = ("zl", "x", "y", "zh", "core")
SIZES = (8, 4, 4, 2, 2)
FACTOR = HEAD_DIM ** (-0.5) * 1.4426950408889634
BLANK = -1e30
F32 = jnp.float32
BF16 = jnp.bfloat16

KV = 768


def route(dx=0, dy=0, dz=0, flip=0, by_core=False):
    pairs = []
    for src in range(512):
        rest, core = divmod(src, 2)
        rest, zh = divmod(rest, 2)
        rest, y = divmod(rest, 4)
        zl, x = divmod(rest, 4)
        sign = -1 if by_core and core else 1
        z = (zh * 8 + zl + sign * dz) % 16
        dst = ((((z % 8) * 4 + (x + dx) % 4) * 4 + (y + dy) % 4) * 2 + z // 8) * 2 + (core ^ flip)
        pairs.append((src, dst))
    return pairs


def move(array, **step):
    return lax.ppermute(array, AXES, route(**step))


def hop(array):
    return move(array, dz=4, by_core=True)


SMEM = pl.BlockSpec(memory_space=pltpu.SMEM)


def shape(*dims, dtype=BF16):
    return jax.ShapeDtypeStruct(dims, dtype)


def whole(*dims):
    return pl.BlockSpec(dims, lambda i: (0,) * len(dims))


FREE = pl.CostEstimate(flops=1, transcendentals=0, bytes_accessed=1)


def params():
    return pltpu.CompilerParams(vmem_limit_bytes=48 * 2**20)


def prep_kernel(
    y_ref, q_hbm, k_hbm, v_hbm, far_out, own_kv, staged, q_out, q_ref, k_ref, v_ref, sems
):
    copies = [
        pltpu.make_async_copy(source, target, sems.at[i])
        for i, (source, target) in enumerate(((k_hbm, k_ref), (v_hbm, v_ref), (q_hbm, q_ref)))
    ]
    for copy in copies:
        copy.start()
    for copy in copies:
        copy.wait()
    keys = k_ref[...]
    keys32 = keys.astype(F32)
    values = v_ref[...].astype(F32)
    values_t = values.T.astype(BF16)
    queries_t = q_ref[...].astype(F32).T.astype(BF16)
    row = lax.broadcasted_iota(jnp.int32, (16, 768), 0)
    chosen = row == lax.broadcasted_iota(jnp.int32, (16, 768), 1) // HEAD_DIM
    picked = [
        jnp.sum(jnp.where(chosen, source[j * R3 : j * R3 + 16], 0.0), axis=0, keepdims=True)
        for source in (keys32, values)
        for j in range(2)
    ]
    packed = []
    for group in range(4):
        lo = group * SPAN
        part = keys32[:, lo : lo + SPAN]
        staged[group, 0:256, :] = part[:, 0:128].astype(BF16)
        staged[group, 256:384, :] = jnp.concatenate(
            [part[0:128, 128:192], part[128:256, 128:192]], axis=1
        ).astype(BF16)
        staged[group, 384:576, :] = values_t[lo : lo + SPAN, 0:128]
        staged[group, 576:768, :] = values_t[lo : lo + SPAN, 128:256]
        q_out[group] = queries_t[lo : lo + SPAN, :]
        far_rows = []
        for first, second in (picked[0:2], picked[2:4]):
            first, second = first[:, lo : lo + SPAN], second[:, lo : lo + SPAN]
            far_rows += [
                first[:, 0:128],
                second[:, 0:128],
                jnp.concatenate([first[:, 128:192], second[:, 128:192]], axis=1),
            ]
        packed += far_rows + [jnp.zeros((2, 128), F32)]
    packed = jnp.concatenate(packed, axis=0).astype(BF16)
    for i in range(16):
        far_out[i] = packed
    own_kv[...] = staged[y_ref[0]]


def prep(y, queries, keys, values):
    shapes = [(16, 32, 128), (KV, 128), (4, KV, 128), (4, SPAN, 256)]
    return pl.pallas_call(
        prep_kernel,
        grid=(1,),
        out_shape=[shape(*dims) for dims in shapes],
        in_specs=[SMEM] + [pl.BlockSpec(memory_space=pltpu.HBM)] * 3,
        out_specs=[whole(*dims) for dims in shapes],
        scratch_shapes=[pltpu.VMEM((256, 768), BF16)] * 3 + [pltpu.SemaphoreType.DMA((3,))],
        compiler_params=params(),
        name="prep",
    )(y, queries, keys, values)


def sort_kernel(y_ref, got, away):
    for i in range(3):
        away[i * KV : (i + 1) * KV, :] = got[lax.rem(y_ref[0] + 1 + i, 4)]


def sort(y, got):
    return pl.pallas_call(
        sort_kernel,
        grid=(1,),
        out_shape=shape(3 * KV, 128),
        in_specs=[SMEM, whole(4, KV, 128)],
        out_specs=whole(3 * KV, 128),
        compiler_params=params(),
        cost_estimate=FREE,
        name="sort",
    )(y, got)


def spread_kernel(rows_ref, out):
    rows = rows_ref[...].astype(F32).reshape(16, 4, 8, 128)
    for group in range(4):
        part = rows[:, group]
        kinds = []
        for base in (0, 3):
            kinds += [part[i, base : base + 2] for i in range(16)]
            kinds += [part[i, base + 2 : base + 3] for i in range(16)]
        packed = jnp.concatenate(kinds, axis=0).astype(BF16)
        for x in range(4):
            for core in range(2):
                out[(x * 4 + group) * 2 + core] = packed


def spread(rows):
    return pl.pallas_call(
        spread_kernel,
        grid=(1,),
        out_shape=shape(32, 96, 128),
        in_specs=[whole(16, 32, 128)],
        out_specs=whole(32, 96, 128),
        compiler_params=params(),
        cost_estimate=FREE,
        name="spread",
    )(rows)


def attend(blocks, queries, head, scores, first_peak):
    mine = queries[head * HEAD_DIM : (head + 1) * HEAD_DIM]
    blank = jnp.zeros_like(mine)
    low = jnp.concatenate([mine, blank], axis=0)
    high = jnp.concatenate([blank, mine], axis=0)
    top = None
    for i, (ref, base) in enumerate(blocks):
        if head < 2:
            parts = [(ref[base : base + 256, :], high if head else low)]
        else:
            third = ref[base + 256 : base + 384, :]
            parts = [(third, low), (third, high)]
        at = i * 256
        for rows, side in parts:
            s = jnp.dot(rows, side, preferred_element_type=F32)
            count = s.shape[0]
            scores[at : at + count, :] = s
            at += count
            here = jnp.max(s.reshape(count // 8, 8, 512), axis=0)
            top = here if top is None else jnp.maximum(top, here)
    peak = jnp.max(top, axis=0, keepdims=True)
    if first_peak is not None:
        peak = jnp.maximum(peak, first_peak)
    total = jnp.zeros((8, 512), F32)
    partial_value = jnp.zeros((HEAD_DIM, 512), F32)
    lo = head * HEAD_DIM
    for i, (ref, base) in enumerate(blocks):
        expos = jnp.exp2((scores[i * 256 : (i + 1) * 256, :] - peak) * FACTOR)
        total = total + jnp.sum(expos.reshape(32, 8, 512), axis=0)
        values = jnp.concatenate(
            [
                ref[base + 384 + lo : base + 384 + lo + HEAD_DIM, :],
                ref[base + 576 + lo : base + 576 + lo + HEAD_DIM, :],
            ],
            axis=1,
        )
        partial_value = partial_value + jnp.dot(
            values, expos.astype(BF16), preferred_element_type=F32
        )
    return peak, jnp.sum(total, axis=0, keepdims=True), partial_value


def near_kernel(counts, has_state, is_last, q_ref, *refs):
    refs = list(refs)
    blocks = []
    for count in counts:
        ref = refs.pop(0)
        blocks += [(ref, i * KV) for i in range(count)]
    if has_state:
        old_sum, old_stat = refs.pop(0), refs.pop(0)
    if is_last:
        far_sum, far_stat = refs.pop(0), refs.pop(0)
        out, scores = refs
    else:
        sum_out, stat_out, scores = refs
    queries = jnp.concatenate([q_ref[0], q_ref[1]], axis=1)
    peaks, totals = [], []
    for head in range(OWN):
        rows = slice(head * HEAD_DIM, (head + 1) * HEAD_DIM)
        first_peak = None
        if has_state:
            old_peak = old_stat[head : head + 1, :]
            old_total = old_stat[4 + head : 5 + head, :]
            first_peak = old_peak
        if is_last:
            far_peak = far_stat[head : head + 1, :]
            far_total = far_stat[8 + head : 9 + head, :]
            first_peak = jnp.maximum(old_peak, far_peak)
        peak, total, partial_value = attend(blocks, queries, head, scores.at[head], first_peak)
        if has_state:
            scale = jnp.exp2((old_peak - peak) * FACTOR)
            total = total + old_total * scale
            partial_value = partial_value + old_sum[rows, :] * scale
        if is_last:
            scale = jnp.exp2((far_peak - peak) * FACTOR)
            total = total + far_total * scale
            partial_value = partial_value + far_sum[rows, :] * scale
            result = (partial_value / total).astype(BF16)
            out[0, rows, :] = result[:, 0:256]
            out[1, rows, :] = result[:, 256:512]
        else:
            sum_out[rows, :] = partial_value
            peaks.append(peak)
            totals.append(total)
    if not is_last:
        blank = [jnp.zeros((1, 512), F32)]
        stat_out[...] = jnp.concatenate(peaks + blank + totals + blank, axis=0)


def near(queries, arrays, state=None, far_state=None):
    def along(rows):
        return pl.BlockSpec((rows, 512), lambda i: (0, i))

    counts = tuple(a.shape[0] // KV for a in arrays)
    is_last = far_state is not None
    two = pl.BlockSpec((2, SPAN, 256), lambda i: (i, 0, 0))
    operands = [queries, *arrays]
    in_specs = [two] + [whole(*a.shape) for a in arrays]
    if state is not None:
        operands += state
        in_specs += [along(SPAN), along(8)]
    if is_last:
        operands += far_state
        in_specs += [along(SPAN), along(16)]
        out_shape, out_specs = shape(4, SPAN, 256), two
    else:
        out_shape = [shape(SPAN, 1024, dtype=F32), shape(8, 1024, dtype=F32)]
        out_specs = [along(SPAN), along(8)]
    return pl.pallas_call(
        functools.partial(near_kernel, counts, state is not None, is_last),
        grid=(2,),
        out_shape=out_shape,
        in_specs=in_specs,
        out_specs=out_specs,
        scratch_shapes=[pltpu.VMEM((OWN, sum(counts) * 256, 512), F32)],
        compiler_params=params(),
        name="last" if is_last else "near",
    )(*operands)


def far_kernel(y_ref, q_ref, rows_ref, sum_out, stat_out):
    y = y_ref[0]
    place_r = lax.broadcasted_iota(jnp.int32, (1024, 128), 1)
    place = ((place_r // 2) % 4) * 256 + (place_r % 2) * 128 + y * OWN + place_r // 8
    lane = lax.broadcasted_iota(jnp.int32, (1024, 128), 0)
    pick = jnp.where((place_r < 24) & (lane == place), 1.0, 0.0)
    chosen = jnp.zeros((SPAN, 128), F32)
    for t in range(4):
        chosen = chosen + jnp.dot(
            q_ref[t], pick[t * 256 : (t + 1) * 256].astype(BF16), preferred_element_type=F32
        )
    row_head = lax.broadcasted_iota(jnp.int32, (SPAN, 128), 0) // HEAD_DIM
    r_head = lax.broadcasted_iota(jnp.int32, (SPAN, 128), 1) // 8
    mine = row_head == r_head
    chosen = jnp.where(mine, chosen, 0.0).astype(BF16)
    third = chosen[128:192]
    blank = jnp.zeros_like(third)

    def section(low, high):
        return rows_ref[:, low:high, :].reshape(32 * (high - low), 128)

    keys_a, keys_b = section(0, 32), section(32, 48)
    values_a = section(48, 80).astype(F32).T.astype(BF16)
    values_b = section(80, 96).astype(F32).T.astype(BF16)
    r = lax.broadcasted_iota(jnp.int32, (1, 128), 1)
    there_a, there_b = r < 16, r >= 16
    scores = [
        jnp.where(there, jnp.dot(rows, side, preferred_element_type=F32), BLANK)
        for rows, side, there in (
            (keys_a, chosen[0:128], there_a),
            (keys_b, jnp.concatenate([third, blank], axis=0), there_b),
            (keys_b, jnp.concatenate([blank, third], axis=0), there_b),
        )
    ]
    peak = functools.reduce(
        jnp.maximum, [jnp.max(s, axis=0, keepdims=True) for s in scores]
    )
    total = jnp.zeros((1, 128), F32)
    sums = []
    for s, values, there in zip(
        scores,
        (values_a, values_b[0:64], values_b[64:128]),
        (there_a, there_b, there_b),
    ):
        expos = jnp.where(there, jnp.exp2((s - peak) * FACTOR), 0.0)
        total = total + jnp.sum(expos, axis=0, keepdims=True)
        sums.append(jnp.dot(values, expos.astype(BF16), preferred_element_type=F32))
    partial_value = jnp.concatenate([sums[0], sums[1] + sums[2]], axis=0)
    partial_value = jnp.where(mine, partial_value, 0.0)
    head = lax.broadcasted_iota(jnp.int32, (8, 128), 0)
    r8 = lax.broadcasted_iota(jnp.int32, (8, 128), 1)
    same = (r8 // 8 == head) & (r8 < 24)
    wide = jnp.concatenate(
        [
            partial_value,
            jnp.where(same, peak, 0.0),
            jnp.where(same, total, 0.0),
            jnp.where(same, 1.0, 0.0),
        ],
        axis=0,
    )
    dense = lax.dot_general(
        wide,
        pick,
        (((1,), (1,)), ((), ())),
        precision=lax.Precision.HIGHEST,
        preferred_element_type=F32,
    )
    sum_out[...] = dense[0:SPAN]
    there = dense[SPAN + 16 : SPAN + 24] > 0.5
    stat_out[0:8, :] = jnp.where(there, dense[SPAN : SPAN + 8], BLANK)
    stat_out[8:16, :] = dense[SPAN + 8 : SPAN + 16]


def far(y, queries, rows):
    return pl.pallas_call(
        far_kernel,
        grid=(1,),
        out_shape=[shape(SPAN, 1024, dtype=F32), shape(16, 1024, dtype=F32)],
        in_specs=[SMEM, whole(4, SPAN, 256), whole(32, 96, 128)],
        out_specs=[whole(SPAN, 1024), whole(16, 1024)],
        compiler_params=params(),
        name="far",
    )(y, queries, rows)


def turn_kernel(in_ref, out_ref):
    out_ref[...] = in_ref[...].astype(F32).T.astype(BF16)


def turn(array):
    return pl.pallas_call(
        turn_kernel,
        grid=(1,),
        out_shape=shape(256, 768),
        in_specs=[whole(768, 256)],
        out_specs=whole(256, 768),
        compiler_params=params(),
        name="turn",
    )(array)


def exchange(y, staged, far_rows):
    far_rows = lax.all_to_all(far_rows, ("zl", "zh"), 0, 0, tiled=True)
    got = lax.all_to_all(staged, "y", 0, 0, tiled=True)
    return got.reshape(4 * KV, 128), sort(y, got), far_rows


def beside(y, q, all_kv, crossed_own, far_rows):
    far_rows = lax.all_to_all(spread(far_rows), ("x", "y", "core"), 0, 0, tiled=True)
    q = lax.all_to_all(q, "y", 0, 0, tiled=True)
    partner_kv = move(all_kv, flip=1)
    partner_own = move(crossed_own, flip=1)
    state = near(q, [all_kv, partner_kv, crossed_own, partner_own])
    far_rows, *state = lax.optimization_barrier((far_rows, *state))
    return q, tuple(state), tuple(far(y, q, far_rows))


def branch(y, work, *args):
    def blank(*args):
        return jax.tree.map(lambda a: jnp.zeros(a.shape, a.dtype), jax.eval_shape(work, *args))

    return lax.cond(y[0] < 4, work, blank, *args)


def body(queries, keys, values):
    y = lax.axis_index("y").astype(jnp.int32).reshape(1)
    far_rows, own_kv, staged, q = prep(y, queries, keys, values)
    crossed_own = move(own_kv, dz=8)
    all_kv, away, far_rows = branch(y, exchange, y, staged, far_rows)
    away, crossed_own = lax.optimization_barrier((away, crossed_own))
    crossed = move(away, dz=8)
    q, state, far_state = branch(y, beside, y, q, all_kv, crossed_own, far_rows)
    crossed, state, far_state = lax.optimization_barrier((crossed, state, far_state))
    partner_crossed = move(crossed, flip=1)
    state = near(q, [crossed], state)
    result = near(q, [partner_crossed], state, far_state)
    back = lax.all_to_all(result, "y", 0, 0, tiled=True)
    return turn(back.reshape(HEADS * HEAD_DIM, 256))


def solution(mesh):
    fine = Mesh(mesh.devices.reshape(SIZES), AXES)
    placed = P(AXES, None)
    return jax.shard_map(
        body, mesh=fine, in_specs=(placed,) * 3, out_specs=placed, check_vma=False
    )
```

```python
import functools

import jax
import jax.numpy as jnp
from jax import lax
from jax.experimental import pallas as pl
from jax.experimental.pallas import tpu as pltpu
from jax.sharding import Mesh
from jax.sharding import PartitionSpec as P

HEADS = 12
HEAD_DIM = 64
R3 = 128
OWN = 3
SPAN = OWN * HEAD_DIM
AXES = ("zl", "x", "y", "zh", "core")
SIZES = (8, 4, 4, 2, 2)
FACTOR = HEAD_DIM ** (-0.5) * 1.4426950408889634
BLANK = -1e30
F32 = jnp.float32
BF16 = jnp.bfloat16

KV = 768


def route(dx=0, dy=0, dz=0, flip=0, by_core=False):
    pairs = []
    for src in range(512):
        rest, core = divmod(src, 2)
        rest, zh = divmod(rest, 2)
        rest, y = divmod(rest, 4)
        zl, x = divmod(rest, 4)
        sign = -1 if by_core and core else 1
        z = (zh * 8 + zl + sign * dz) % 16
        dst = ((((z % 8) * 4 + (x + dx) % 4) * 4 + (y + dy) % 4) * 2 + z // 8) * 2 + (core ^ flip)
        pairs.append((src, dst))
    return pairs


def move(array, **step):
    return lax.ppermute(array, AXES, route(**step))


def hop(array):
    return move(array, dz=4, by_core=True)


SMEM = pl.BlockSpec(memory_space=pltpu.SMEM)


def shape(*dims, dtype=BF16):
    return jax.ShapeDtypeStruct(dims, dtype)


def whole(*dims):
    return pl.BlockSpec(dims, lambda i: (0,) * len(dims))


FREE = pl.CostEstimate(flops=1, transcendentals=0, bytes_accessed=1)


def params():
    return pltpu.CompilerParams(vmem_limit_bytes=48 * 2**20)


def prep_kernel(
    y_ref, q_hbm, k_hbm, v_hbm, far_out, own_kv, staged, q_out, q_ref, k_ref, v_ref, sems
):
    copies = [
        pltpu.make_async_copy(source, target, sems.at[i])
        for i, (source, target) in enumerate(((k_hbm, k_ref), (v_hbm, v_ref), (q_hbm, q_ref)))
    ]
    for copy in copies:
        copy.start()
    for copy in copies:
        copy.wait()
    keys = k_ref[...]
    keys32 = keys.astype(F32)
    values = v_ref[...].astype(F32)
    values_t = values.T.astype(BF16)
    queries_t = q_ref[...].astype(F32).T.astype(BF16)
    row = lax.broadcasted_iota(jnp.int32, (16, 768), 0)
    chosen = row == lax.broadcasted_iota(jnp.int32, (16, 768), 1) // HEAD_DIM
    picked = [
        jnp.sum(jnp.where(chosen, source[j * R3 : j * R3 + 16], 0.0), axis=0, keepdims=True)
        for source in (keys32, values)
        for j in range(2)
    ]
    packed = []
    for group in range(4):
        lo = group * SPAN
        part = keys32[:, lo : lo + SPAN]
        staged[group, 0:256, :] = part[:, 0:128].astype(BF16)
        staged[group, 256:384, :] = jnp.concatenate(
            [part[0:128, 128:192], part[128:256, 128:192]], axis=1
        ).astype(BF16)
        staged[group, 384:576, :] = values_t[lo : lo + SPAN, 0:128]
        staged[group, 576:768, :] = values_t[lo : lo + SPAN, 128:256]
        q_out[group] = queries_t[lo : lo + SPAN, :]
        far_rows = []
        for first, second in (picked[0:2], picked[2:4]):
            first, second = first[:, lo : lo + SPAN], second[:, lo : lo + SPAN]
            far_rows += [
                first[:, 0:128],
                second[:, 0:128],
                jnp.concatenate([first[:, 128:192], second[:, 128:192]], axis=1),
            ]
        packed += far_rows + [jnp.zeros((2, 128), F32)]
    packed = jnp.concatenate(packed, axis=0).astype(BF16)
    for i in range(16):
        far_out[i] = packed
    own_kv[...] = staged[y_ref[0]]


def prep(y, queries, keys, values):
    shapes = [(16, 32, 128), (KV, 128), (4, KV, 128), (4, SPAN, 256)]
    return pl.pallas_call(
        prep_kernel,
        grid=(1,),
        out_shape=[shape(*dims) for dims in shapes],
        in_specs=[SMEM] + [pl.BlockSpec(memory_space=pltpu.HBM)] * 3,
        out_specs=[whole(*dims) for dims in shapes],
        scratch_shapes=[pltpu.VMEM((256, 768), BF16)] * 3 + [pltpu.SemaphoreType.DMA((3,))],
        compiler_params=params(),
        name="prep",
    )(y, queries, keys, values)


def sort_kernel(y_ref, got, away):
    for i in range(3):
        away[i * KV : (i + 1) * KV, :] = got[lax.rem(y_ref[0] + 1 + i, 4)]


def sort(y, got):
    return pl.pallas_call(
        sort_kernel,
        grid=(1,),
        out_shape=shape(3 * KV, 128),
        in_specs=[SMEM, whole(4, KV, 128)],
        out_specs=whole(3 * KV, 128),
        compiler_params=params(),
        cost_estimate=FREE,
        name="sort",
    )(y, got)


def spread_kernel(rows_ref, out):
    rows = rows_ref[...].astype(F32).reshape(16, 4, 8, 128)
    for group in range(4):
        part = rows[:, group]
        kinds = []
        for base in (0, 3):
            kinds += [part[i, base : base + 2] for i in range(16)]
            kinds += [part[i, base + 2 : base + 3] for i in range(16)]
        packed = jnp.concatenate(kinds, axis=0).astype(BF16)
        for x in range(4):
            for core in range(2):
                out[(x * 4 + group) * 2 + core] = packed


def spread(rows):
    return pl.pallas_call(
        spread_kernel,
        grid=(1,),
        out_shape=shape(32, 96, 128),
        in_specs=[whole(16, 32, 128)],
        out_specs=whole(32, 96, 128),
        compiler_params=params(),
        cost_estimate=FREE,
        name="spread",
    )(rows)


def attend(blocks, queries, head, scores, first_peak):
    mine = queries[head * HEAD_DIM : (head + 1) * HEAD_DIM]
    blank = jnp.zeros_like(mine)
    low = jnp.concatenate([mine, blank], axis=0)
    high = jnp.concatenate([blank, mine], axis=0)
    top = None
    for i, (ref, base) in enumerate(blocks):
        if head < 2:
            parts = [(ref[base : base + 256, :], high if head else low)]
        else:
            third = ref[base + 256 : base + 384, :]
            parts = [(third, low), (third, high)]
        at = i * 256
        for rows, side in parts:
            s = jnp.dot(rows, side, preferred_element_type=F32)
            count = s.shape[0]
            scores[at : at + count, :] = s
            at += count
            here = jnp.max(s.reshape(count // 8, 8, 512), axis=0)
            top = here if top is None else jnp.maximum(top, here)
    peak = jnp.max(top, axis=0, keepdims=True)
    if first_peak is not None:
        peak = jnp.maximum(peak, first_peak)
    total = jnp.zeros((8, 512), F32)
    partial_value = jnp.zeros((HEAD_DIM, 512), F32)
    lo = head * HEAD_DIM
    for i, (ref, base) in enumerate(blocks):
        expos = jnp.exp2((scores[i * 256 : (i + 1) * 256, :] - peak) * FACTOR)
        total = total + jnp.sum(expos.reshape(32, 8, 512), axis=0)
        values = jnp.concatenate(
            [
                ref[base + 384 + lo : base + 384 + lo + HEAD_DIM, :],
                ref[base + 576 + lo : base + 576 + lo + HEAD_DIM, :],
            ],
            axis=1,
        )
        partial_value = partial_value + jnp.dot(
            values, expos.astype(BF16), preferred_element_type=F32
        )
    return peak, jnp.sum(total, axis=0, keepdims=True), partial_value


def near_kernel(counts, has_state, is_last, q_ref, *refs):
    refs = list(refs)
    blocks = []
    for count in counts:
        ref = refs.pop(0)
        blocks += [(ref, i * KV) for i in range(count)]
    if has_state:
        old_sum, old_stat = refs.pop(0), refs.pop(0)
    if is_last:
        far_sum, far_stat = refs.pop(0), refs.pop(0)
        out, scores = refs
    else:
        sum_out, stat_out, scores = refs
    queries = jnp.concatenate([q_ref[0], q_ref[1]], axis=1)
    peaks, totals = [], []
    for head in range(OWN):
        rows = slice(head * HEAD_DIM, (head + 1) * HEAD_DIM)
        first_peak = None
        if has_state:
            old_peak = old_stat[head : head + 1, :]
            old_total = old_stat[4 + head : 5 + head, :]
            first_peak = old_peak
        if is_last:
            far_peak = far_stat[head : head + 1, :]
            far_total = far_stat[8 + head : 9 + head, :]
            first_peak = jnp.maximum(old_peak, far_peak)
        peak, total, partial_value = attend(blocks, queries, head, scores.at[head], first_peak)
        if has_state:
            scale = jnp.exp2((old_peak - peak) * FACTOR)
            total = total + old_total * scale
            partial_value = partial_value + old_sum[rows, :] * scale
        if is_last:
            scale = jnp.exp2((far_peak - peak) * FACTOR)
            total = total + far_total * scale
            partial_value = partial_value + far_sum[rows, :] * scale
            result = (partial_value / total).astype(BF16)
            out[0, rows, :] = result[:, 0:256]
            out[1, rows, :] = result[:, 256:512]
        else:
            sum_out[rows, :] = partial_value
            peaks.append(peak)
            totals.append(total)
    if not is_last:
        blank = [jnp.zeros((1, 512), F32)]
        stat_out[...] = jnp.concatenate(peaks + blank + totals + blank, axis=0)


def near(queries, arrays, state=None, far_state=None):
    def along(rows):
        return pl.BlockSpec((rows, 512), lambda i: (0, i))

    counts = tuple(a.shape[0] // KV for a in arrays)
    is_last = far_state is not None
    two = pl.BlockSpec((2, SPAN, 256), lambda i: (i, 0, 0))
    operands = [queries, *arrays]
    in_specs = [two] + [whole(*a.shape) for a in arrays]
    if state is not None:
        operands += state
        in_specs += [along(SPAN), along(8)]
    if is_last:
        operands += far_state
        in_specs += [along(SPAN), along(16)]
        out_shape, out_specs = shape(4, SPAN, 256), two
    else:
        out_shape = [shape(SPAN, 1024, dtype=F32), shape(8, 1024, dtype=F32)]
        out_specs = [along(SPAN), along(8)]
    return pl.pallas_call(
        functools.partial(near_kernel, counts, state is not None, is_last),
        grid=(2,),
        out_shape=out_shape,
        in_specs=in_specs,
        out_specs=out_specs,
        scratch_shapes=[pltpu.VMEM((OWN, sum(counts) * 256, 512), F32)],
        compiler_params=params(),
        name="last" if is_last else "near",
    )(*operands)


def far_kernel(y_ref, q_ref, rows_ref, sum_out, stat_out):
    y = y_ref[0]
    place_r = lax.broadcasted_iota(jnp.int32, (1024, 128), 1)
    place = ((place_r // 2) % 4) * 256 + (place_r % 2) * 128 + y * OWN + place_r // 8
    lane = lax.broadcasted_iota(jnp.int32, (1024, 128), 0)
    pick = jnp.where((place_r < 24) & (lane == place), 1.0, 0.0)
    chosen = jnp.zeros((SPAN, 128), F32)
    for t in range(4):
        chosen = chosen + jnp.dot(
            q_ref[t], pick[t * 256 : (t + 1) * 256].astype(BF16), preferred_element_type=F32
        )
    row_head = lax.broadcasted_iota(jnp.int32, (SPAN, 128), 0) // HEAD_DIM
    r_head = lax.broadcasted_iota(jnp.int32, (SPAN, 128), 1) // 8
    mine = row_head == r_head
    chosen = jnp.where(mine, chosen, 0.0).astype(BF16)
    third = chosen[128:192]
    blank = jnp.zeros_like(third)

    def section(low, high):
        return rows_ref[:, low:high, :].reshape(32 * (high - low), 128)

    keys_a, keys_b = section(0, 32), section(32, 48)
    values_a = section(48, 80).astype(F32).T.astype(BF16)
    values_b = section(80, 96).astype(F32).T.astype(BF16)
    r = lax.broadcasted_iota(jnp.int32, (1, 128), 1)
    there_a, there_b = r < 16, r >= 16
    scores = [
        jnp.where(there, jnp.dot(rows, side, preferred_element_type=F32), BLANK)
        for rows, side, there in (
            (keys_a, chosen[0:128], there_a),
            (keys_b, jnp.concatenate([third, blank], axis=0), there_b),
            (keys_b, jnp.concatenate([blank, third], axis=0), there_b),
        )
    ]
    peak = functools.reduce(
        jnp.maximum, [jnp.max(s, axis=0, keepdims=True) for s in scores]
    )
    total = jnp.zeros((1, 128), F32)
    sums = []
    for s, values, there in zip(
        scores,
        (values_a, values_b[0:64], values_b[64:128]),
        (there_a, there_b, there_b),
    ):
        expos = jnp.where(there, jnp.exp2((s - peak) * FACTOR), 0.0)
        total = total + jnp.sum(expos, axis=0, keepdims=True)
        sums.append(jnp.dot(values, expos.astype(BF16), preferred_element_type=F32))
    partial_value = jnp.concatenate([sums[0], sums[1] + sums[2]], axis=0)
    partial_value = jnp.where(mine, partial_value, 0.0)
    head = lax.broadcasted_iota(jnp.int32, (8, 128), 0)
    r8 = lax.broadcasted_iota(jnp.int32, (8, 128), 1)
    same = (r8 // 8 == head) & (r8 < 24)
    wide = jnp.concatenate(
        [
            partial_value,
            jnp.where(same, peak, 0.0),
            jnp.where(same, total, 0.0),
            jnp.where(same, 1.0, 0.0),
        ],
        axis=0,
    )
    dense = lax.dot_general(
        wide,
        pick,
        (((1,), (1,)), ((), ())),
        precision=lax.Precision.HIGHEST,
        preferred_element_type=F32,
    )
    sum_out[...] = dense[0:SPAN]
    there = dense[SPAN + 16 : SPAN + 24] > 0.5
    stat_out[0:8, :] = jnp.where(there, dense[SPAN : SPAN + 8], BLANK)
    stat_out[8:16, :] = dense[SPAN + 8 : SPAN + 16]


def far(y, queries, rows):
    return pl.pallas_call(
        far_kernel,
        grid=(1,),
        out_shape=[shape(SPAN, 1024, dtype=F32), shape(16, 1024, dtype=F32)],
        in_specs=[SMEM, whole(4, SPAN, 256), whole(32, 96, 128)],
        out_specs=[whole(SPAN, 1024), whole(16, 1024)],
        compiler_params=params(),
        name="far",
    )(y, queries, rows)


def turn_kernel(in_ref, out_ref):
    out_ref[...] = in_ref[...].astype(F32).T.astype(BF16)


def turn(array):
    return pl.pallas_call(
        turn_kernel,
        grid=(1,),
        out_shape=shape(256, 768),
        in_specs=[whole(768, 256)],
        out_specs=whole(256, 768),
        compiler_params=params(),
        name="turn",
    )(array)


def exchange(y, staged, far_rows):
    far_rows = spread(far_rows)
    got = lax.all_to_all(staged, "y", 0, 0, tiled=True)
    return got.reshape(4 * KV, 128), sort(y, got), far_rows


def beside(y, q, all_kv, crossed_own, far_rows):
    far_rows = lax.all_to_all(far_rows, ("x", "y", "core"), 0, 0, tiled=True)
    q = lax.all_to_all(q, "y", 0, 0, tiled=True)
    partner_kv = move(all_kv, flip=1)
    partner_own = move(crossed_own, flip=1)
    state = near(q, [all_kv, partner_kv, crossed_own, partner_own])
    far_rows, *state = lax.optimization_barrier((far_rows, *state))
    return q, tuple(state), tuple(far(y, q, far_rows))


def branch(y, work, *args):
    def blank(*args):
        return jax.tree.map(lambda a: jnp.zeros(a.shape, a.dtype), jax.eval_shape(work, *args))

    return lax.cond(y[0] < 4, work, blank, *args)


def body(queries, keys, values):
    y = lax.axis_index("y").astype(jnp.int32).reshape(1)
    queries, keys, values = (
        pltpu.with_memory_space_constraint(a, pltpu.HBM) for a in (queries, keys, values)
    )
    far_rows, own_kv, staged, q = prep(y, queries, keys, values)
    far_rows = lax.all_to_all(far_rows, ("zl", "zh"), 0, 0, tiled=True)
    crossed_own = move(own_kv, dz=8)
    all_kv, away, far_rows = branch(y, exchange, y, staged, far_rows)
    away, crossed_own = lax.optimization_barrier((away, crossed_own))
    crossed = move(away, dz=8)
    q, state, far_state = branch(y, beside, y, q, all_kv, crossed_own, far_rows)
    crossed, state, far_state = lax.optimization_barrier((crossed, state, far_state))
    partner_crossed = move(crossed, flip=1)
    state = near(q, [crossed], state)
    result = near(q, [partner_crossed], state, far_state)
    back = lax.all_to_all(result, "y", 0, 0, tiled=True)
    return turn(back.reshape(HEADS * HEAD_DIM, 256))


def solution(mesh):
    fine = Mesh(mesh.devices.reshape(SIZES), AXES)
    placed = P(AXES, None)
    return jax.shard_map(
        body, mesh=fine, in_specs=(placed,) * 3, out_specs=placed, check_vma=False
    )
```

```python
import functools

import jax
import jax.numpy as jnp
from jax import lax
from jax.experimental import pallas as pl
from jax.experimental.pallas import tpu as pltpu
from jax.sharding import Mesh
from jax.sharding import PartitionSpec as P

HEADS = 12
HEAD_DIM = 64
R3 = 128
OWN = 3
SPAN = OWN * HEAD_DIM
AXES = ("zl", "x", "y", "zh", "core")
SIZES = (8, 4, 4, 2, 2)
FACTOR = HEAD_DIM ** (-0.5) * 1.4426950408889634
BLANK = -1e30
F32 = jnp.float32
BF16 = jnp.bfloat16

KV = 768


def route(dx=0, dy=0, dz=0, flip=0, by_core=False):
    pairs = []
    for src in range(512):
        rest, core = divmod(src, 2)
        rest, zh = divmod(rest, 2)
        rest, y = divmod(rest, 4)
        zl, x = divmod(rest, 4)
        sign = -1 if by_core and core else 1
        z = (zh * 8 + zl + sign * dz) % 16
        dst = ((((z % 8) * 4 + (x + dx) % 4) * 4 + (y + dy) % 4) * 2 + z // 8) * 2 + (core ^ flip)
        pairs.append((src, dst))
    return pairs


def move(array, **step):
    return lax.ppermute(array, AXES, route(**step))


def hop(array):
    return move(array, dz=4, by_core=True)


SMEM = pl.BlockSpec(memory_space=pltpu.SMEM)


def shape(*dims, dtype=BF16):
    return jax.ShapeDtypeStruct(dims, dtype)


def whole(*dims):
    return pl.BlockSpec(dims, lambda i: (0,) * len(dims))


FREE = pl.CostEstimate(flops=1, transcendentals=0, bytes_accessed=1)


def params():
    return pltpu.CompilerParams(vmem_limit_bytes=48 * 2**20)


def prep_kernel(
    y_ref, q_hbm, k_hbm, v_hbm, far_out, own_kv, staged, q_out, q_ref, k_ref, v_ref, sems
):
    copies = [
        pltpu.make_async_copy(source, target, sems.at[i])
        for i, (source, target) in enumerate(((k_hbm, k_ref), (v_hbm, v_ref), (q_hbm, q_ref)))
    ]
    for copy in copies:
        copy.start()
    for copy in copies:
        copy.wait()
    keys = k_ref[...]
    keys32 = keys.astype(F32)
    values = v_ref[...].astype(F32)
    values_t = values.T.astype(BF16)
    queries_t = q_ref[...].astype(F32).T.astype(BF16)
    row = lax.broadcasted_iota(jnp.int32, (16, 768), 0)
    chosen = row == lax.broadcasted_iota(jnp.int32, (16, 768), 1) // HEAD_DIM
    picked = [
        jnp.sum(jnp.where(chosen, source[j * R3 : j * R3 + 16], 0.0), axis=0, keepdims=True)
        for source in (keys32, values)
        for j in range(2)
    ]
    packed = []
    for group in range(4):
        lo = group * SPAN
        part = keys32[:, lo : lo + SPAN]
        staged[group, 0:256, :] = part[:, 0:128].astype(BF16)
        staged[group, 256:384, :] = jnp.concatenate(
            [part[0:128, 128:192], part[128:256, 128:192]], axis=1
        ).astype(BF16)
        staged[group, 384:576, :] = values_t[lo : lo + SPAN, 0:128]
        staged[group, 576:768, :] = values_t[lo : lo + SPAN, 128:256]
        q_out[group] = queries_t[lo : lo + SPAN, :]
        far_rows = []
        for first, second in (picked[0:2], picked[2:4]):
            first, second = first[:, lo : lo + SPAN], second[:, lo : lo + SPAN]
            far_rows += [
                first[:, 0:128],
                second[:, 0:128],
                jnp.concatenate([first[:, 128:192], second[:, 128:192]], axis=1),
            ]
        packed += far_rows + [jnp.zeros((2, 128), F32)]
    packed = jnp.concatenate(packed, axis=0).astype(BF16)
    for i in range(16):
        far_out[i] = packed
    own_kv[...] = staged[y_ref[0]]


def prep(y, queries, keys, values):
    shapes = [(16, 32, 128), (KV, 128), (4, KV, 128), (4, SPAN, 256)]
    return pl.pallas_call(
        prep_kernel,
        grid=(1,),
        out_shape=[shape(*dims) for dims in shapes],
        in_specs=[SMEM] + [pl.BlockSpec(memory_space=pltpu.HBM)] * 3,
        out_specs=[whole(*dims) for dims in shapes],
        scratch_shapes=[pltpu.VMEM((256, 768), BF16)] * 3 + [pltpu.SemaphoreType.DMA((3,))],
        compiler_params=params(),
        name="prep",
    )(y, queries, keys, values)


def sort_kernel(y_ref, got, away):
    for i in range(3):
        away[i * KV : (i + 1) * KV, :] = got[lax.rem(y_ref[0] + 1 + i, 4)]


def sort(y, got):
    return pl.pallas_call(
        sort_kernel,
        grid=(1,),
        out_shape=shape(3 * KV, 128),
        in_specs=[SMEM, whole(4, KV, 128)],
        out_specs=whole(3 * KV, 128),
        compiler_params=params(),
        cost_estimate=FREE,
        name="sort",
    )(y, got)


def spread_kernel(rows_ref, out):
    rows = rows_ref[...].astype(F32).reshape(16, 4, 8, 128)
    for group in range(4):
        part = rows[:, group]
        kinds = []
        for base in (0, 3):
            kinds += [part[i, base : base + 2] for i in range(16)]
            kinds += [part[i, base + 2 : base + 3] for i in range(16)]
        packed = jnp.concatenate(kinds, axis=0).astype(BF16)
        for x in range(4):
            for core in range(2):
                out[(x * 4 + group) * 2 + core] = packed


def spread(rows):
    return pl.pallas_call(
        spread_kernel,
        grid=(1,),
        out_shape=shape(32, 96, 128),
        in_specs=[whole(16, 32, 128)],
        out_specs=whole(32, 96, 128),
        compiler_params=params(),
        cost_estimate=FREE,
        name="spread",
    )(rows)


def attend(blocks, queries, head, scores, first_peak):
    mine = queries[head * HEAD_DIM : (head + 1) * HEAD_DIM]
    blank = jnp.zeros_like(mine)
    low = jnp.concatenate([mine, blank], axis=0)
    high = jnp.concatenate([blank, mine], axis=0)
    top = None
    for i, (ref, base) in enumerate(blocks):
        if head < 2:
            parts = [(ref[base : base + 256, :], high if head else low)]
        else:
            third = ref[base + 256 : base + 384, :]
            parts = [(third, low), (third, high)]
        at = i * 256
        for rows, side in parts:
            s = jnp.dot(rows, side, preferred_element_type=F32)
            count = s.shape[0]
            scores[at : at + count, :] = s
            at += count
            here = jnp.max(s.reshape(count // 8, 8, 512), axis=0)
            top = here if top is None else jnp.maximum(top, here)
    peak = jnp.max(top, axis=0, keepdims=True)
    if first_peak is not None:
        peak = jnp.maximum(peak, first_peak)
    total = jnp.zeros((8, 512), F32)
    partial_value = jnp.zeros((HEAD_DIM, 512), F32)
    lo = head * HEAD_DIM
    for i, (ref, base) in enumerate(blocks):
        expos = jnp.exp2((scores[i * 256 : (i + 1) * 256, :] - peak) * FACTOR)
        total = total + jnp.sum(expos.reshape(32, 8, 512), axis=0)
        values = jnp.concatenate(
            [
                ref[base + 384 + lo : base + 384 + lo + HEAD_DIM, :],
                ref[base + 576 + lo : base + 576 + lo + HEAD_DIM, :],
            ],
            axis=1,
        )
        partial_value = partial_value + jnp.dot(
            values, expos.astype(BF16), preferred_element_type=F32
        )
    return peak, jnp.sum(total, axis=0, keepdims=True), partial_value


def near_kernel(counts, has_state, is_last, q_ref, *refs):
    refs = list(refs)
    blocks = []
    for count in counts:
        ref = refs.pop(0)
        blocks += [(ref, i * KV) for i in range(count)]
    if has_state:
        old_sum, old_stat = refs.pop(0), refs.pop(0)
    if is_last:
        far_sum, far_stat = refs.pop(0), refs.pop(0)
        out, scores = refs
    else:
        sum_out, stat_out, scores = refs
    queries = jnp.concatenate([q_ref[0], q_ref[1]], axis=1)
    peaks, totals = [], []
    for head in range(OWN):
        rows = slice(head * HEAD_DIM, (head + 1) * HEAD_DIM)
        first_peak = None
        if has_state:
            old_peak = old_stat[head : head + 1, :]
            old_total = old_stat[4 + head : 5 + head, :]
            first_peak = old_peak
        if is_last:
            far_peak = far_stat[head : head + 1, :]
            far_total = far_stat[8 + head : 9 + head, :]
            first_peak = jnp.maximum(old_peak, far_peak)
        peak, total, partial_value = attend(blocks, queries, head, scores.at[head], first_peak)
        if has_state:
            scale = jnp.exp2((old_peak - peak) * FACTOR)
            total = total + old_total * scale
            partial_value = partial_value + old_sum[rows, :] * scale
        if is_last:
            scale = jnp.exp2((far_peak - peak) * FACTOR)
            total = total + far_total * scale
            partial_value = partial_value + far_sum[rows, :] * scale
            result = (partial_value / total).astype(BF16)
            out[0, rows, :] = result[:, 0:256]
            out[1, rows, :] = result[:, 256:512]
        else:
            sum_out[rows, :] = partial_value
            peaks.append(peak)
            totals.append(total)
    if not is_last:
        blank = [jnp.zeros((1, 512), F32)]
        stat_out[...] = jnp.concatenate(peaks + blank + totals + blank, axis=0)


def near(queries, arrays, state=None, far_state=None):
    def along(rows):
        return pl.BlockSpec((rows, 512), lambda i: (0, i))

    counts = tuple(a.shape[0] // KV for a in arrays)
    is_last = far_state is not None
    two = pl.BlockSpec((2, SPAN, 256), lambda i: (i, 0, 0))
    operands = [queries, *arrays]
    in_specs = [two] + [whole(*a.shape) for a in arrays]
    if state is not None:
        operands += state
        in_specs += [along(SPAN), along(8)]
    if is_last:
        operands += far_state
        in_specs += [along(SPAN), along(16)]
        out_shape, out_specs = shape(4, SPAN, 256), two
    else:
        out_shape = [shape(SPAN, 1024, dtype=F32), shape(8, 1024, dtype=F32)]
        out_specs = [along(SPAN), along(8)]
    return pl.pallas_call(
        functools.partial(near_kernel, counts, state is not None, is_last),
        grid=(2,),
        out_shape=out_shape,
        in_specs=in_specs,
        out_specs=out_specs,
        scratch_shapes=[pltpu.VMEM((OWN, sum(counts) * 256, 512), F32)],
        compiler_params=params(),
        name="last" if is_last else "near",
    )(*operands)


def far_kernel(y_ref, q_ref, rows_ref, sum_out, stat_out):
    y = y_ref[0]
    place_r = lax.broadcasted_iota(jnp.int32, (1024, 128), 1)
    place = ((place_r // 2) % 4) * 256 + (place_r % 2) * 128 + y * OWN + place_r // 8
    lane = lax.broadcasted_iota(jnp.int32, (1024, 128), 0)
    pick = jnp.where((place_r < 24) & (lane == place), 1.0, 0.0)
    chosen = jnp.zeros((SPAN, 128), F32)
    for t in range(4):
        chosen = chosen + jnp.dot(
            q_ref[t], pick[t * 256 : (t + 1) * 256].astype(BF16), preferred_element_type=F32
        )
    row_head = lax.broadcasted_iota(jnp.int32, (SPAN, 128), 0) // HEAD_DIM
    r_head = lax.broadcasted_iota(jnp.int32, (SPAN, 128), 1) // 8
    mine = row_head == r_head
    chosen = jnp.where(mine, chosen, 0.0).astype(BF16)
    third = chosen[128:192]
    blank = jnp.zeros_like(third)

    def section(low, high):
        return rows_ref[:, low:high, :].reshape(32 * (high - low), 128)

    keys_a, keys_b = section(0, 32), section(32, 48)
    values_a = section(48, 80).astype(F32).T.astype(BF16)
    values_b = section(80, 96).astype(F32).T.astype(BF16)
    r = lax.broadcasted_iota(jnp.int32, (1, 128), 1)
    there_a, there_b = r < 16, r >= 16
    scores = [
        jnp.where(there, jnp.dot(rows, side, preferred_element_type=F32), BLANK)
        for rows, side, there in (
            (keys_a, chosen[0:128], there_a),
            (keys_b, jnp.concatenate([third, blank], axis=0), there_b),
            (keys_b, jnp.concatenate([blank, third], axis=0), there_b),
        )
    ]
    peak = functools.reduce(
        jnp.maximum, [jnp.max(s, axis=0, keepdims=True) for s in scores]
    )
    total = jnp.zeros((1, 128), F32)
    sums = []
    for s, values, there in zip(
        scores,
        (values_a, values_b[0:64], values_b[64:128]),
        (there_a, there_b, there_b),
    ):
        expos = jnp.where(there, jnp.exp2((s - peak) * FACTOR), 0.0)
        total = total + jnp.sum(expos, axis=0, keepdims=True)
        sums.append(jnp.dot(values, expos.astype(BF16), preferred_element_type=F32))
    partial_value = jnp.concatenate([sums[0], sums[1] + sums[2]], axis=0)
    partial_value = jnp.where(mine, partial_value, 0.0)
    head = lax.broadcasted_iota(jnp.int32, (8, 128), 0)
    r8 = lax.broadcasted_iota(jnp.int32, (8, 128), 1)
    same = (r8 // 8 == head) & (r8 < 24)
    wide = jnp.concatenate(
        [
            partial_value,
            jnp.where(same, peak, 0.0),
            jnp.where(same, total, 0.0),
            jnp.where(same, 1.0, 0.0),
        ],
        axis=0,
    )
    dense = lax.dot_general(
        wide,
        pick,
        (((1,), (1,)), ((), ())),
        precision=lax.Precision.HIGHEST,
        preferred_element_type=F32,
    )
    sum_out[...] = dense[0:SPAN]
    there = dense[SPAN + 16 : SPAN + 24] > 0.5
    stat_out[0:8, :] = jnp.where(there, dense[SPAN : SPAN + 8], BLANK)
    stat_out[8:16, :] = dense[SPAN + 8 : SPAN + 16]


def far(y, queries, rows):
    return pl.pallas_call(
        far_kernel,
        grid=(1,),
        out_shape=[shape(SPAN, 1024, dtype=F32), shape(16, 1024, dtype=F32)],
        in_specs=[SMEM, whole(4, SPAN, 256), whole(32, 96, 128)],
        out_specs=[whole(SPAN, 1024), whole(16, 1024)],
        compiler_params=params(),
        name="far",
    )(y, queries, rows)


def turn_kernel(in_ref, out_ref):
    out_ref[...] = in_ref[...].astype(F32).T.astype(BF16)


def turn(array):
    return pl.pallas_call(
        turn_kernel,
        grid=(1,),
        out_shape=shape(256, 768),
        in_specs=[whole(768, 256)],
        out_specs=whole(256, 768),
        compiler_params=params(),
        name="turn",
    )(array)


def exchange(y, staged, far_rows):
    far_rows = spread(far_rows)
    got = lax.all_to_all(staged, "y", 0, 0, tiled=True)
    return got.reshape(4 * KV, 128), sort(y, got), far_rows


def beside(y, q, all_kv, crossed_own, far_rows):
    far_rows = lax.all_to_all(far_rows, ("x", "y", "core"), 0, 0, tiled=True)
    q = lax.all_to_all(q, "y", 0, 0, tiled=True)
    partner_kv = move(all_kv, flip=1)
    partner_own = move(crossed_own, flip=1)
    state = near(q, [all_kv, partner_kv, crossed_own, partner_own])
    far_rows, *state = lax.optimization_barrier((far_rows, *state))
    return q, tuple(state), tuple(far(y, q, far_rows))


def branch(y, work, *args):
    def blank(*args):
        return jax.tree.map(lambda a: jnp.zeros(a.shape, a.dtype), jax.eval_shape(work, *args))

    return lax.cond(y[0] < 4, work, blank, *args)


def body(queries, keys, values):
    y = lax.axis_index("y").astype(jnp.int32).reshape(1)
    queries, keys, values = (
        pltpu.with_memory_space_constraint(a, pltpu.HBM) for a in (queries, keys, values)
    )
    far_rows, own_kv, staged, q = prep(y, queries, keys, values)
    far_rows = lax.all_to_all(far_rows, ("zl", "zh"), 0, 0, tiled=True)
    far_rows, own_kv, staged = lax.optimization_barrier((far_rows, own_kv, staged))
    crossed_own = move(own_kv, dz=8)
    all_kv, away, far_rows = branch(y, exchange, y, staged, far_rows)
    away, crossed_own = lax.optimization_barrier((away, crossed_own))
    crossed = move(away, dz=8)
    q, state, far_state = branch(y, beside, y, q, all_kv, crossed_own, far_rows)
    crossed, state, far_state = lax.optimization_barrier((crossed, state, far_state))
    partner_crossed = move(crossed, flip=1)
    state = near(q, [crossed], state)
    result = near(q, [partner_crossed], state, far_state)
    back = lax.all_to_all(result, "y", 0, 0, tiled=True)
    return turn(back.reshape(HEADS * HEAD_DIM, 256))


def solution(mesh):
    fine = Mesh(mesh.devices.reshape(SIZES), AXES)
    placed = P(AXES, None)
    return jax.shard_map(
        body, mesh=fine, in_specs=(placed,) * 3, out_specs=placed, check_vma=False
    )
```

```python
import functools

import jax
import jax.numpy as jnp
from jax import lax
from jax.experimental import pallas as pl
from jax.experimental.pallas import tpu as pltpu
from jax.sharding import Mesh
from jax.sharding import PartitionSpec as P

HEADS = 12
HEAD_DIM = 64
R3 = 128
OWN = 3
SPAN = OWN * HEAD_DIM
AXES = ("zl", "x", "y", "zh", "core")
SIZES = (8, 4, 4, 2, 2)
FACTOR = HEAD_DIM ** (-0.5) * 1.4426950408889634
BLANK = -1e30
F32 = jnp.float32
BF16 = jnp.bfloat16

KV = 768


def route(dx=0, dy=0, dz=0, flip=0, by_core=False):
    pairs = []
    for src in range(512):
        rest, core = divmod(src, 2)
        rest, zh = divmod(rest, 2)
        rest, y = divmod(rest, 4)
        zl, x = divmod(rest, 4)
        sign = -1 if by_core and core else 1
        z = (zh * 8 + zl + sign * dz) % 16
        dst = ((((z % 8) * 4 + (x + dx) % 4) * 4 + (y + dy) % 4) * 2 + z // 8) * 2 + (core ^ flip)
        pairs.append((src, dst))
    return pairs


def move(array, **step):
    return lax.ppermute(array, AXES, route(**step))


def hop(array):
    return move(array, dz=4, by_core=True)


SMEM = pl.BlockSpec(memory_space=pltpu.SMEM)


def shape(*dims, dtype=BF16):
    return jax.ShapeDtypeStruct(dims, dtype)


def whole(*dims):
    return pl.BlockSpec(dims, lambda i: (0,) * len(dims))


FREE = pl.CostEstimate(flops=1, transcendentals=0, bytes_accessed=1)


def params():
    return pltpu.CompilerParams(vmem_limit_bytes=48 * 2**20)


def prep_kernel(
    q_hbm, k_hbm, v_hbm, far_out, staged, q_out, q_ref, k_ref, v_ref, sems
):
    copies = [
        pltpu.make_async_copy(source, target, sems.at[i])
        for i, (source, target) in enumerate(((k_hbm, k_ref), (v_hbm, v_ref), (q_hbm, q_ref)))
    ]
    for copy in copies:
        copy.start()
    for copy in copies:
        copy.wait()
    keys = k_ref[...]
    keys32 = keys.astype(F32)
    values = v_ref[...].astype(F32)
    values_t = values.T.astype(BF16)
    queries_t = q_ref[...].astype(F32).T.astype(BF16)
    row = lax.broadcasted_iota(jnp.int32, (16, 768), 0)
    chosen = row == lax.broadcasted_iota(jnp.int32, (16, 768), 1) // HEAD_DIM
    picked = [
        jnp.sum(jnp.where(chosen, source[j * R3 : j * R3 + 16], 0.0), axis=0, keepdims=True)
        for source in (keys32, values)
        for j in range(2)
    ]
    packed = []
    for group in range(4):
        lo = group * SPAN
        part = keys32[:, lo : lo + SPAN]
        staged[group, 0:256, :] = part[:, 0:128].astype(BF16)
        staged[group, 256:384, :] = jnp.concatenate(
            [part[0:128, 128:192], part[128:256, 128:192]], axis=1
        ).astype(BF16)
        staged[group, 384:576, :] = values_t[lo : lo + SPAN, 0:128]
        staged[group, 576:768, :] = values_t[lo : lo + SPAN, 128:256]
        q_out[group] = queries_t[lo : lo + SPAN, :]
        far_rows = []
        for first, second in (picked[0:2], picked[2:4]):
            first, second = first[:, lo : lo + SPAN], second[:, lo : lo + SPAN]
            far_rows += [
                first[:, 0:128],
                second[:, 0:128],
                jnp.concatenate([first[:, 128:192], second[:, 128:192]], axis=1),
            ]
        packed += far_rows + [jnp.zeros((2, 128), F32)]
    far_out[...] = jnp.concatenate(packed, axis=0).astype(BF16)


def prep(queries, keys, values):
    shapes = [(32, 128), (4, KV, 128), (4, SPAN, 256)]
    return pl.pallas_call(
        prep_kernel,
        grid=(1,),
        out_shape=[shape(*dims) for dims in shapes],
        in_specs=[pl.BlockSpec(memory_space=pltpu.HBM)] * 3,
        out_specs=[whole(*dims) for dims in shapes],
        scratch_shapes=[pltpu.VMEM((256, 768), BF16)] * 3 + [pltpu.SemaphoreType.DMA((3,))],
        compiler_params=params(),
        name="prep",
    )(queries, keys, values)


def spread_kernel(rows_ref, out):
    rows = rows_ref[...].astype(F32).reshape(16, 4, 8, 128)
    for group in range(4):
        part = rows[:, group]
        kinds = []
        for base in (0, 3):
            kinds += [part[i, base : base + 2] for i in range(16)]
            kinds += [part[i, base + 2 : base + 3] for i in range(16)]
        packed = jnp.concatenate(kinds, axis=0).astype(BF16)
        for x in range(4):
            for core in range(2):
                out[(x * 4 + group) * 2 + core] = packed


def spread(rows):
    return pl.pallas_call(
        spread_kernel,
        grid=(1,),
        out_shape=shape(32, 96, 128),
        in_specs=[whole(512, 128)],
        out_specs=whole(32, 96, 128),
        compiler_params=params(),
        cost_estimate=FREE,
        name="spread",
    )(rows)


def attend(blocks, queries, head, scores, first_peak):
    mine = queries[head * HEAD_DIM : (head + 1) * HEAD_DIM]
    blank = jnp.zeros_like(mine)
    low = jnp.concatenate([mine, blank], axis=0)
    high = jnp.concatenate([blank, mine], axis=0)
    top = None
    for i, (ref, base) in enumerate(blocks):
        if head < 2:
            parts = [(ref[base : base + 256, :], high if head else low)]
        else:
            third = ref[base + 256 : base + 384, :]
            parts = [(third, low), (third, high)]
        at = i * 256
        for rows, side in parts:
            s = jnp.dot(rows, side, preferred_element_type=F32)
            count = s.shape[0]
            scores[at : at + count, :] = s
            at += count
            here = jnp.max(s.reshape(count // 8, 8, 512), axis=0)
            top = here if top is None else jnp.maximum(top, here)
    peak = jnp.max(top, axis=0, keepdims=True)
    if first_peak is not None:
        peak = jnp.maximum(peak, first_peak)
    total = jnp.zeros((8, 512), F32)
    partial_value = jnp.zeros((HEAD_DIM, 512), F32)
    lo = head * HEAD_DIM
    for i, (ref, base) in enumerate(blocks):
        expos = jnp.exp2((scores[i * 256 : (i + 1) * 256, :] - peak) * FACTOR)
        total = total + jnp.sum(expos.reshape(32, 8, 512), axis=0)
        values = jnp.concatenate(
            [
                ref[base + 384 + lo : base + 384 + lo + HEAD_DIM, :],
                ref[base + 576 + lo : base + 576 + lo + HEAD_DIM, :],
            ],
            axis=1,
        )
        partial_value = partial_value + jnp.dot(
            values, expos.astype(BF16), preferred_element_type=F32
        )
    return peak, jnp.sum(total, axis=0, keepdims=True), partial_value


def near_kernel(counts, has_state, is_last, q_ref, *refs):
    refs = list(refs)
    blocks = []
    for count in counts:
        ref = refs.pop(0)
        blocks += [(ref, i * KV) for i in range(count)]
    if has_state:
        old_sum, old_stat = refs.pop(0), refs.pop(0)
    if is_last:
        far_sum, far_stat = refs.pop(0), refs.pop(0)
        out, scores = refs
    else:
        sum_out, stat_out, scores = refs
    queries = jnp.concatenate([q_ref[0], q_ref[1]], axis=1)
    peaks, totals = [], []
    for head in range(OWN):
        rows = slice(head * HEAD_DIM, (head + 1) * HEAD_DIM)
        first_peak = None
        if has_state:
            old_peak = old_stat[head : head + 1, :]
            old_total = old_stat[4 + head : 5 + head, :]
            first_peak = old_peak
        if is_last:
            far_peak = far_stat[head : head + 1, :]
            far_total = far_stat[8 + head : 9 + head, :]
            first_peak = jnp.maximum(old_peak, far_peak)
        peak, total, partial_value = attend(blocks, queries, head, scores.at[head], first_peak)
        if has_state:
            scale = jnp.exp2((old_peak - peak) * FACTOR)
            total = total + old_total * scale
            partial_value = partial_value + old_sum[rows, :] * scale
        if is_last:
            scale = jnp.exp2((far_peak - peak) * FACTOR)
            total = total + far_total * scale
            partial_value = partial_value + far_sum[rows, :] * scale
            result = (partial_value / total).astype(BF16)
            out[0, rows, :] = result[:, 0:256]
            out[1, rows, :] = result[:, 256:512]
        else:
            sum_out[rows, :] = partial_value
            peaks.append(peak)
            totals.append(total)
    if not is_last:
        blank = [jnp.zeros((1, 512), F32)]
        stat_out[...] = jnp.concatenate(peaks + blank + totals + blank, axis=0)


def near(queries, arrays, state=None, far_state=None):
    def along(rows):
        return pl.BlockSpec((rows, 512), lambda i: (0, i))

    counts = tuple(a.shape[0] // KV for a in arrays)
    is_last = far_state is not None
    two = pl.BlockSpec((2, SPAN, 256), lambda i: (i, 0, 0))
    operands = [queries, *arrays]
    in_specs = [two] + [whole(*a.shape) for a in arrays]
    if state is not None:
        operands += state
        in_specs += [along(SPAN), along(8)]
    if is_last:
        operands += far_state
        in_specs += [along(SPAN), along(16)]
        out_shape, out_specs = shape(4, SPAN, 256), two
    else:
        out_shape = [shape(SPAN, 1024, dtype=F32), shape(8, 1024, dtype=F32)]
        out_specs = [along(SPAN), along(8)]
    return pl.pallas_call(
        functools.partial(near_kernel, counts, state is not None, is_last),
        grid=(2,),
        out_shape=out_shape,
        in_specs=in_specs,
        out_specs=out_specs,
        scratch_shapes=[pltpu.VMEM((OWN, sum(counts) * 256, 512), F32)],
        compiler_params=params(),
        name="last" if is_last else "near",
    )(*operands)


def far_kernel(y_ref, q_ref, rows_ref, sum_out, stat_out):
    y = y_ref[0]
    place_r = lax.broadcasted_iota(jnp.int32, (1024, 128), 1)
    place = ((place_r // 2) % 4) * 256 + (place_r % 2) * 128 + y * OWN + place_r // 8
    lane = lax.broadcasted_iota(jnp.int32, (1024, 128), 0)
    pick = jnp.where((place_r < 24) & (lane == place), 1.0, 0.0)
    chosen = jnp.zeros((SPAN, 128), F32)
    for t in range(4):
        chosen = chosen + jnp.dot(
            q_ref[t], pick[t * 256 : (t + 1) * 256].astype(BF16), preferred_element_type=F32
        )
    row_head = lax.broadcasted_iota(jnp.int32, (SPAN, 128), 0) // HEAD_DIM
    r_head = lax.broadcasted_iota(jnp.int32, (SPAN, 128), 1) // 8
    mine = row_head == r_head
    chosen = jnp.where(mine, chosen, 0.0).astype(BF16)
    third = chosen[128:192]
    blank = jnp.zeros_like(third)

    def section(low, high):
        return rows_ref[:, low:high, :].reshape(32 * (high - low), 128)

    keys_a, keys_b = section(0, 32), section(32, 48)
    values_a = section(48, 80).astype(F32).T.astype(BF16)
    values_b = section(80, 96).astype(F32).T.astype(BF16)
    r = lax.broadcasted_iota(jnp.int32, (1, 128), 1)
    there_a, there_b = r < 16, r >= 16
    scores = [
        jnp.where(there, jnp.dot(rows, side, preferred_element_type=F32), BLANK)
        for rows, side, there in (
            (keys_a, chosen[0:128], there_a),
            (keys_b, jnp.concatenate([third, blank], axis=0), there_b),
            (keys_b, jnp.concatenate([blank, third], axis=0), there_b),
        )
    ]
    peak = functools.reduce(
        jnp.maximum, [jnp.max(s, axis=0, keepdims=True) for s in scores]
    )
    total = jnp.zeros((1, 128), F32)
    sums = []
    for s, values, there in zip(
        scores,
        (values_a, values_b[0:64], values_b[64:128]),
        (there_a, there_b, there_b),
    ):
        expos = jnp.where(there, jnp.exp2((s - peak) * FACTOR), 0.0)
        total = total + jnp.sum(expos, axis=0, keepdims=True)
        sums.append(jnp.dot(values, expos.astype(BF16), preferred_element_type=F32))
    partial_value = jnp.concatenate([sums[0], sums[1] + sums[2]], axis=0)
    partial_value = jnp.where(mine, partial_value, 0.0)
    head = lax.broadcasted_iota(jnp.int32, (8, 128), 0)
    r8 = lax.broadcasted_iota(jnp.int32, (8, 128), 1)
    same = (r8 // 8 == head) & (r8 < 24)
    wide = jnp.concatenate(
        [
            partial_value,
            jnp.where(same, peak, 0.0),
            jnp.where(same, total, 0.0),
            jnp.where(same, 1.0, 0.0),
        ],
        axis=0,
    )
    dense = lax.dot_general(
        wide,
        pick,
        (((1,), (1,)), ((), ())),
        precision=lax.Precision.HIGHEST,
        preferred_element_type=F32,
    )
    sum_out[...] = dense[0:SPAN]
    there = dense[SPAN + 16 : SPAN + 24] > 0.5
    stat_out[0:8, :] = jnp.where(there, dense[SPAN : SPAN + 8], BLANK)
    stat_out[8:16, :] = dense[SPAN + 8 : SPAN + 16]


def far(y, queries, rows):
    return pl.pallas_call(
        far_kernel,
        grid=(1,),
        out_shape=[shape(SPAN, 1024, dtype=F32), shape(16, 1024, dtype=F32)],
        in_specs=[SMEM, whole(4, SPAN, 256), whole(32, 96, 128)],
        out_specs=[whole(SPAN, 1024), whole(16, 1024)],
        compiler_params=params(),
        name="far",
    )(y, queries, rows)


def turn_kernel(in_ref, out_ref):
    out_ref[...] = in_ref[...].astype(F32).T.astype(BF16)


def turn(array):
    return pl.pallas_call(
        turn_kernel,
        grid=(1,),
        out_shape=shape(256, 768),
        in_specs=[whole(768, 256)],
        out_specs=whole(256, 768),
        compiler_params=params(),
        name="turn",
    )(array)


def double(rows, dz):
    return jnp.concatenate([rows, move(rows, dz=dz)], axis=0)


def exchange(staged, far_rows):
    got = lax.all_to_all(staged, "y", 0, 0, tiled=True)
    for dz in (1, -2, 4, 8):
        far_rows = double(far_rows, dz)
    return got.reshape(4 * KV, 128), far_rows


def beside(y, q, all_kv, far_rows):
    far_rows = lax.all_to_all(spread(far_rows), ("x", "y", "core"), 0, 0, tiled=True)
    q = lax.all_to_all(q, "y", 0, 0, tiled=True)
    partner_kv = move(all_kv, flip=1)
    state = near(q, [all_kv, partner_kv])
    far_rows, *state = lax.optimization_barrier((far_rows, *state))
    return q, tuple(state), tuple(far(y, q, far_rows))


def branch(y, work, *args):
    def blank(*args):
        return jax.tree.map(lambda a: jnp.zeros(a.shape, a.dtype), jax.eval_shape(work, *args))

    return lax.cond(y[0] < 4, work, blank, *args)


def body(queries, keys, values):
    y = lax.axis_index("y").astype(jnp.int32).reshape(1)
    queries, keys, values = (
        pltpu.with_memory_space_constraint(a, pltpu.HBM) for a in (queries, keys, values)
    )
    far_rows, staged, q = prep(queries, keys, values)
    all_kv, far_rows = branch(y, exchange, staged, far_rows)
    crossed = move(all_kv, dz=8)
    q, state, far_state = branch(y, beside, y, q, all_kv, far_rows)
    crossed, state, far_state = lax.optimization_barrier((crossed, state, far_state))
    partner_crossed = move(crossed, flip=1)
    state = near(q, [crossed], state)
    result = near(q, [partner_crossed], state, far_state)
    back = lax.all_to_all(result, "y", 0, 0, tiled=True)
    return turn(back.reshape(HEADS * HEAD_DIM, 256))


def solution(mesh):
    fine = Mesh(mesh.devices.reshape(SIZES), AXES)
    placed = P(AXES, None)
    return jax.shard_map(
        body, mesh=fine, in_specs=(placed,) * 3, out_specs=placed, check_vma=False
    )
```

```python
import functools

import jax
import jax.numpy as jnp
from jax import lax
from jax.experimental import pallas as pl
from jax.experimental.pallas import tpu as pltpu
from jax.sharding import Mesh
from jax.sharding import PartitionSpec as P

HEADS = 12
HEAD_DIM = 64
R3 = 128
OWN = 3
SPAN = OWN * HEAD_DIM
AXES = ("zl", "x", "y", "zh", "core")
SIZES = (8, 4, 4, 2, 2)
FACTOR = HEAD_DIM ** (-0.5) * 1.4426950408889634
BLANK = -1e30
F32 = jnp.float32
BF16 = jnp.bfloat16

KV = 768


def route(dx=0, dy=0, dz=0, flip=0, by_core=False):
    pairs = []
    for src in range(512):
        rest, core = divmod(src, 2)
        rest, zh = divmod(rest, 2)
        rest, y = divmod(rest, 4)
        zl, x = divmod(rest, 4)
        sign = -1 if by_core and core else 1
        z = (zh * 8 + zl + sign * dz) % 16
        dst = ((((z % 8) * 4 + (x + dx) % 4) * 4 + (y + dy) % 4) * 2 + z // 8) * 2 + (core ^ flip)
        pairs.append((src, dst))
    return pairs


def move(array, **step):
    return lax.ppermute(array, AXES, route(**step))


def hop(array):
    return move(array, dz=4, by_core=True)


SMEM = pl.BlockSpec(memory_space=pltpu.SMEM)


def shape(*dims, dtype=BF16):
    return jax.ShapeDtypeStruct(dims, dtype)


def whole(*dims):
    return pl.BlockSpec(dims, lambda i: (0,) * len(dims))


FREE = pl.CostEstimate(flops=1, transcendentals=0, bytes_accessed=1)


def params():
    return pltpu.CompilerParams(vmem_limit_bytes=48 * 2**20)


def prep_kernel(
    y_ref, q_hbm, k_hbm, v_hbm, far_out, own_kv, staged, q_out, q_ref, k_ref, v_ref, sems
):
    copies = [
        pltpu.make_async_copy(source, target, sems.at[i])
        for i, (source, target) in enumerate(((k_hbm, k_ref), (v_hbm, v_ref), (q_hbm, q_ref)))
    ]
    for copy in copies:
        copy.start()
    for copy in copies:
        copy.wait()
    keys = k_ref[...]
    keys32 = keys.astype(F32)
    values = v_ref[...].astype(F32)
    values_t = values.T.astype(BF16)
    queries_t = q_ref[...].astype(F32).T.astype(BF16)
    row = lax.broadcasted_iota(jnp.int32, (16, 768), 0)
    chosen = row == lax.broadcasted_iota(jnp.int32, (16, 768), 1) // HEAD_DIM
    picked = [
        jnp.sum(jnp.where(chosen, source[j * R3 : j * R3 + 16], 0.0), axis=0, keepdims=True)
        for source in (keys32, values)
        for j in range(2)
    ]
    packed = []
    for group in range(4):
        lo = group * SPAN
        part = keys32[:, lo : lo + SPAN]
        staged[group, 0:256, :] = part[:, 0:128].astype(BF16)
        staged[group, 256:384, :] = jnp.concatenate(
            [part[0:128, 128:192], part[128:256, 128:192]], axis=1
        ).astype(BF16)
        staged[group, 384:576, :] = values_t[lo : lo + SPAN, 0:128]
        staged[group, 576:768, :] = values_t[lo : lo + SPAN, 128:256]
        q_out[group] = queries_t[lo : lo + SPAN, :]
        far_rows = []
        for first, second in (picked[0:2], picked[2:4]):
            first, second = first[:, lo : lo + SPAN], second[:, lo : lo + SPAN]
            far_rows += [
                first[:, 0:128],
                second[:, 0:128],
                jnp.concatenate([first[:, 128:192], second[:, 128:192]], axis=1),
            ]
        packed += far_rows + [jnp.zeros((2, 128), F32)]
    packed = jnp.concatenate(packed, axis=0).astype(BF16)
    for i in range(16):
        far_out[i] = packed
    own_kv[...] = staged[y_ref[0]]


def prep(y, queries, keys, values):
    shapes = [(16, 32, 128), (KV, 128), (4, KV, 128), (4, SPAN, 256)]
    return pl.pallas_call(
        prep_kernel,
        grid=(1,),
        out_shape=[shape(*dims) for dims in shapes],
        in_specs=[SMEM] + [pl.BlockSpec(memory_space=pltpu.HBM)] * 3,
        out_specs=[whole(*dims) for dims in shapes],
        scratch_shapes=[pltpu.VMEM((256, 768), BF16)] * 3 + [pltpu.SemaphoreType.DMA((3,))],
        compiler_params=params(),
        name="prep",
    )(y, queries, keys, values)


def sort_kernel(y_ref, got, away):
    for i in range(3):
        away[i * KV : (i + 1) * KV, :] = got[lax.rem(y_ref[0] + 1 + i, 4)]


def sort(y, got):
    return pl.pallas_call(
        sort_kernel,
        grid=(1,),
        out_shape=shape(3 * KV, 128),
        in_specs=[SMEM, whole(4, KV, 128)],
        out_specs=whole(3 * KV, 128),
        compiler_params=params(),
        cost_estimate=FREE,
        name="sort",
    )(y, got)


def spread_kernel(rows_ref, out):
    rows = rows_ref[...].astype(F32).reshape(16, 4, 8, 128)
    for group in range(4):
        part = rows[:, group]
        kinds = []
        for base in (0, 3):
            kinds += [part[i, base : base + 2] for i in range(16)]
            kinds += [part[i, base + 2 : base + 3] for i in range(16)]
        packed = jnp.concatenate(kinds, axis=0).astype(BF16)
        for x in range(4):
            for core in range(2):
                out[(x * 4 + group) * 2 + core] = packed


def spread(rows):
    return pl.pallas_call(
        spread_kernel,
        grid=(1,),
        out_shape=shape(32, 96, 128),
        in_specs=[whole(16, 32, 128)],
        out_specs=whole(32, 96, 128),
        compiler_params=params(),
        cost_estimate=FREE,
        name="spread",
    )(rows)


def attend(blocks, queries, head, scores, first_peak):
    mine = queries[head * HEAD_DIM : (head + 1) * HEAD_DIM]
    blank = jnp.zeros_like(mine)
    low = jnp.concatenate([mine, blank], axis=0)
    high = jnp.concatenate([blank, mine], axis=0)
    top = None
    for i, (ref, base) in enumerate(blocks):
        if head < 2:
            parts = [(ref[base : base + 256, :], high if head else low)]
        else:
            third = ref[base + 256 : base + 384, :]
            parts = [(third, low), (third, high)]
        at = i * 256
        for rows, side in parts:
            s = jnp.dot(rows, side, preferred_element_type=F32)
            count = s.shape[0]
            scores[at : at + count, :] = s
            at += count
            here = jnp.max(s.reshape(count // 8, 8, 512), axis=0)
            top = here if top is None else jnp.maximum(top, here)
    peak = jnp.max(top, axis=0, keepdims=True)
    if first_peak is not None:
        peak = jnp.maximum(peak, first_peak)
    total = jnp.zeros((8, 512), F32)
    partial_value = jnp.zeros((HEAD_DIM, 512), F32)
    lo = head * HEAD_DIM
    for i, (ref, base) in enumerate(blocks):
        expos = jnp.exp2((scores[i * 256 : (i + 1) * 256, :] - peak) * FACTOR)
        total = total + jnp.sum(expos.reshape(32, 8, 512), axis=0)
        values = jnp.concatenate(
            [
                ref[base + 384 + lo : base + 384 + lo + HEAD_DIM, :],
                ref[base + 576 + lo : base + 576 + lo + HEAD_DIM, :],
            ],
            axis=1,
        )
        partial_value = partial_value + jnp.dot(
            values, expos.astype(BF16), preferred_element_type=F32
        )
    return peak, jnp.sum(total, axis=0, keepdims=True), partial_value


def near_kernel(counts, has_state, is_last, q_ref, *refs):
    refs = list(refs)
    blocks = []
    for count in counts:
        ref = refs.pop(0)
        blocks += [(ref, i * KV) for i in range(count)]
    if has_state:
        old_sum, old_stat = refs.pop(0), refs.pop(0)
    if is_last:
        far_sum, far_stat = refs.pop(0), refs.pop(0)
        out, scores = refs
    else:
        sum_out, stat_out, scores = refs
    queries = jnp.concatenate([q_ref[0], q_ref[1]], axis=1)
    peaks, totals = [], []
    for head in range(OWN):
        rows = slice(head * HEAD_DIM, (head + 1) * HEAD_DIM)
        first_peak = None
        if has_state:
            old_peak = old_stat[head : head + 1, :]
            old_total = old_stat[4 + head : 5 + head, :]
            first_peak = old_peak
        if is_last:
            far_peak = far_stat[head : head + 1, :]
            far_total = far_stat[8 + head : 9 + head, :]
            first_peak = jnp.maximum(old_peak, far_peak)
        peak, total, partial_value = attend(blocks, queries, head, scores.at[head], first_peak)
        if has_state:
            scale = jnp.exp2((old_peak - peak) * FACTOR)
            total = total + old_total * scale
            partial_value = partial_value + old_sum[rows, :] * scale
        if is_last:
            scale = jnp.exp2((far_peak - peak) * FACTOR)
            total = total + far_total * scale
            partial_value = partial_value + far_sum[rows, :] * scale
            result = (partial_value / total).astype(BF16)
            out[0, rows, :] = result[:, 0:256]
            out[1, rows, :] = result[:, 256:512]
        else:
            sum_out[rows, :] = partial_value
            peaks.append(peak)
            totals.append(total)
    if not is_last:
        blank = [jnp.zeros((1, 512), F32)]
        stat_out[...] = jnp.concatenate(peaks + blank + totals + blank, axis=0)


def near(queries, arrays, state=None, far_state=None):
    def along(rows):
        return pl.BlockSpec((rows, 512), lambda i: (0, i))

    counts = tuple(a.shape[0] // KV for a in arrays)
    is_last = far_state is not None
    two = pl.BlockSpec((2, SPAN, 256), lambda i: (i, 0, 0))
    operands = [queries, *arrays]
    in_specs = [two] + [whole(*a.shape) for a in arrays]
    if state is not None:
        operands += state
        in_specs += [along(SPAN), along(8)]
    if is_last:
        operands += far_state
        in_specs += [along(SPAN), along(16)]
        out_shape, out_specs = shape(4, SPAN, 256), two
    else:
        out_shape = [shape(SPAN, 1024, dtype=F32), shape(8, 1024, dtype=F32)]
        out_specs = [along(SPAN), along(8)]
    return pl.pallas_call(
        functools.partial(near_kernel, counts, state is not None, is_last),
        grid=(2,),
        out_shape=out_shape,
        in_specs=in_specs,
        out_specs=out_specs,
        scratch_shapes=[pltpu.VMEM((OWN, sum(counts) * 256, 512), F32)],
        compiler_params=params(),
        name="last" if is_last else "near",
    )(*operands)


def far_kernel(y_ref, q_ref, rows_ref, sum_out, stat_out):
    y = y_ref[0]
    place_r = lax.broadcasted_iota(jnp.int32, (1024, 128), 1)
    place = ((place_r // 2) % 4) * 256 + (place_r % 2) * 128 + y * OWN + place_r // 8
    lane = lax.broadcasted_iota(jnp.int32, (1024, 128), 0)
    pick = jnp.where((place_r < 24) & (lane == place), 1.0, 0.0)
    chosen = jnp.zeros((SPAN, 128), F32)
    for t in range(4):
        chosen = chosen + jnp.dot(
            q_ref[t], pick[t * 256 : (t + 1) * 256].astype(BF16), preferred_element_type=F32
        )
    row_head = lax.broadcasted_iota(jnp.int32, (SPAN, 128), 0) // HEAD_DIM
    r_head = lax.broadcasted_iota(jnp.int32, (SPAN, 128), 1) // 8
    mine = row_head == r_head
    chosen = jnp.where(mine, chosen, 0.0).astype(BF16)
    third = chosen[128:192]
    blank = jnp.zeros_like(third)

    def section(low, high):
        return rows_ref[:, low:high, :].reshape(32 * (high - low), 128)

    keys_a, keys_b = section(0, 32), section(32, 48)
    values_a = section(48, 80).astype(F32).T.astype(BF16)
    values_b = section(80, 96).astype(F32).T.astype(BF16)
    r = lax.broadcasted_iota(jnp.int32, (1, 128), 1)
    there_a, there_b = r < 16, r >= 16
    scores = [
        jnp.where(there, jnp.dot(rows, side, preferred_element_type=F32), BLANK)
        for rows, side, there in (
            (keys_a, chosen[0:128], there_a),
            (keys_b, jnp.concatenate([third, blank], axis=0), there_b),
            (keys_b, jnp.concatenate([blank, third], axis=0), there_b),
        )
    ]
    peak = functools.reduce(
        jnp.maximum, [jnp.max(s, axis=0, keepdims=True) for s in scores]
    )
    total = jnp.zeros((1, 128), F32)
    sums = []
    for s, values, there in zip(
        scores,
        (values_a, values_b[0:64], values_b[64:128]),
        (there_a, there_b, there_b),
    ):
        expos = jnp.where(there, jnp.exp2((s - peak) * FACTOR), 0.0)
        total = total + jnp.sum(expos, axis=0, keepdims=True)
        sums.append(jnp.dot(values, expos.astype(BF16), preferred_element_type=F32))
    partial_value = jnp.concatenate([sums[0], sums[1] + sums[2]], axis=0)
    partial_value = jnp.where(mine, partial_value, 0.0)
    head = lax.broadcasted_iota(jnp.int32, (8, 128), 0)
    r8 = lax.broadcasted_iota(jnp.int32, (8, 128), 1)
    same = (r8 // 8 == head) & (r8 < 24)
    wide = jnp.concatenate(
        [
            partial_value,
            jnp.where(same, peak, 0.0),
            jnp.where(same, total, 0.0),
            jnp.where(same, 1.0, 0.0),
        ],
        axis=0,
    )
    dense = lax.dot_general(
        wide,
        pick,
        (((1,), (1,)), ((), ())),
        precision=lax.Precision.HIGHEST,
        preferred_element_type=F32,
    )
    sum_out[...] = dense[0:SPAN]
    there = dense[SPAN + 16 : SPAN + 24] > 0.5
    stat_out[0:8, :] = jnp.where(there, dense[SPAN : SPAN + 8], BLANK)
    stat_out[8:16, :] = dense[SPAN + 8 : SPAN + 16]


def far(y, queries, rows):
    return pl.pallas_call(
        far_kernel,
        grid=(1,),
        out_shape=[shape(SPAN, 1024, dtype=F32), shape(16, 1024, dtype=F32)],
        in_specs=[SMEM, whole(4, SPAN, 256), whole(32, 96, 128)],
        out_specs=[whole(SPAN, 1024), whole(16, 1024)],
        compiler_params=params(),
        name="far",
    )(y, queries, rows)


def turn_kernel(in_ref, out_ref):
    out_ref[...] = in_ref[...].astype(F32).T.astype(BF16)


def turn(array):
    return pl.pallas_call(
        turn_kernel,
        grid=(1,),
        out_shape=shape(256, 768),
        in_specs=[whole(768, 256)],
        out_specs=whole(256, 768),
        compiler_params=params(),
        name="turn",
    )(array)


def exchange(y, staged, far_rows):
    far_rows = lax.all_to_all(far_rows, ("zl", "zh"), 0, 0, tiled=True)
    got = lax.all_to_all(staged, "y", 0, 0, tiled=True)
    return got.reshape(4 * KV, 128), sort(y, got), far_rows


def beside(y, q, all_kv, crossed_own, far_rows):
    far_rows = lax.all_to_all(spread(far_rows), ("x", "y", "core"), 0, 0, tiled=True)
    q = lax.all_to_all(q, "y", 0, 0, tiled=True)
    partner_kv = move(all_kv, flip=1)
    partner_own = move(crossed_own, flip=1)
    state = near(q, [all_kv, partner_kv, crossed_own, partner_own])
    far_rows, *state = lax.optimization_barrier((far_rows, *state))
    return q, tuple(state), tuple(far(y, q, far_rows))


def branch(y, work, *args):
    def blank(*args):
        return jax.tree.map(lambda a: jnp.zeros(a.shape, a.dtype), jax.eval_shape(work, *args))

    return lax.cond(y[0] < 4, work, blank, *args)


def body(queries, keys, values):
    y = lax.axis_index("y").astype(jnp.int32).reshape(1)
    queries, keys, values = (
        pltpu.with_memory_space_constraint(a, pltpu.HBM) for a in (queries, keys, values)
    )
    far_rows, own_kv, staged, q = prep(y, queries, keys, values)
    crossed_own = move(own_kv, dz=8)
    all_kv, away, far_rows = branch(y, exchange, y, staged, far_rows)
    away, crossed_own = lax.optimization_barrier((away, crossed_own))
    crossed = move(away, dz=8)
    q, state, far_state = branch(y, beside, y, q, all_kv, crossed_own, far_rows)
    crossed, state, far_state = lax.optimization_barrier((crossed, state, far_state))
    partner_crossed = move(crossed, flip=1)
    state = near(q, [crossed], state)
    result = near(q, [partner_crossed], state, far_state)
    back = lax.all_to_all(result, "y", 0, 0, tiled=True)
    return turn(back.reshape(HEADS * HEAD_DIM, 256))


def solution(mesh):
    fine = Mesh(mesh.devices.reshape(SIZES), AXES)
    placed = P(AXES, None)
    return jax.shard_map(
        body, mesh=fine, in_specs=(placed,) * 3, out_specs=placed, check_vma=False
    )
```

```python
import functools

import jax
import jax.numpy as jnp
from jax import lax
from jax.experimental import pallas as pl
from jax.experimental.pallas import tpu as pltpu
from jax.sharding import Mesh
from jax.sharding import PartitionSpec as P

HEADS = 12
HEAD_DIM = 64
R3 = 128
OWN = 3
SPAN = OWN * HEAD_DIM
AXES = ("zl", "x", "y", "zh", "core")
SIZES = (8, 4, 4, 2, 2)
FACTOR = HEAD_DIM ** (-0.5) * 1.4426950408889634
BLANK = -1e30
F32 = jnp.float32
BF16 = jnp.bfloat16

KV = 768


def route(dx=0, dy=0, dz=0, flip=0, by_core=False):
    pairs = []
    for src in range(512):
        rest, core = divmod(src, 2)
        rest, zh = divmod(rest, 2)
        rest, y = divmod(rest, 4)
        zl, x = divmod(rest, 4)
        sign = -1 if by_core and core else 1
        z = (zh * 8 + zl + sign * dz) % 16
        dst = ((((z % 8) * 4 + (x + dx) % 4) * 4 + (y + dy) % 4) * 2 + z // 8) * 2 + (core ^ flip)
        pairs.append((src, dst))
    return pairs


def move(array, **step):
    return lax.ppermute(array, AXES, route(**step))


def hop(array):
    return move(array, dz=4, by_core=True)


SMEM = pl.BlockSpec(memory_space=pltpu.SMEM)


def shape(*dims, dtype=BF16):
    return jax.ShapeDtypeStruct(dims, dtype)


def whole(*dims):
    return pl.BlockSpec(dims, lambda i: (0,) * len(dims))


FREE = pl.CostEstimate(flops=1, transcendentals=0, bytes_accessed=1)


def params():
    return pltpu.CompilerParams(vmem_limit_bytes=48 * 2**20)


def prep_kernel(
    y_ref, q_hbm, k_hbm, v_hbm, far_out, own_kv, staged, q_out, q_ref, k_ref, v_ref, sems
):
    copies = [
        pltpu.make_async_copy(source, target, sems.at[i])
        for i, (source, target) in enumerate(((k_hbm, k_ref), (v_hbm, v_ref), (q_hbm, q_ref)))
    ]
    for copy in copies:
        copy.start()
    for copy in copies:
        copy.wait()
    keys = k_ref[...]
    keys32 = keys.astype(F32)
    values = v_ref[...].astype(F32)
    values_t = values.T.astype(BF16)
    queries_t = q_ref[...].astype(F32).T.astype(BF16)
    row = lax.broadcasted_iota(jnp.int32, (16, 768), 0)
    chosen = row == lax.broadcasted_iota(jnp.int32, (16, 768), 1) // HEAD_DIM
    picked = [
        jnp.sum(jnp.where(chosen, source[j * R3 : j * R3 + 16], 0.0), axis=0, keepdims=True)
        for source in (keys32, values)
        for j in range(2)
    ]
    packed = []
    for group in range(4):
        lo = group * SPAN
        part = keys32[:, lo : lo + SPAN]
        staged[group, 0:256, :] = part[:, 0:128].astype(BF16)
        staged[group, 256:384, :] = jnp.concatenate(
            [part[0:128, 128:192], part[128:256, 128:192]], axis=1
        ).astype(BF16)
        staged[group, 384:576, :] = values_t[lo : lo + SPAN, 0:128]
        staged[group, 576:768, :] = values_t[lo : lo + SPAN, 128:256]
        q_out[group] = queries_t[lo : lo + SPAN, :]
        far_rows = []
        for first, second in (picked[0:2], picked[2:4]):
            first, second = first[:, lo : lo + SPAN], second[:, lo : lo + SPAN]
            far_rows += [
                first[:, 0:128],
                second[:, 0:128],
                jnp.concatenate([first[:, 128:192], second[:, 128:192]], axis=1),
            ]
        packed += far_rows + [jnp.zeros((2, 128), F32)]
    packed = jnp.concatenate(packed, axis=0).astype(BF16)
    for i in range(16):
        far_out[i] = packed
    own_kv[...] = staged[y_ref[0]]


def prep(y, queries, keys, values):
    shapes = [(16, 32, 128), (KV, 128), (4, KV, 128), (4, SPAN, 256)]
    return pl.pallas_call(
        prep_kernel,
        grid=(1,),
        out_shape=[shape(*dims) for dims in shapes],
        in_specs=[SMEM] + [pl.BlockSpec(memory_space=pltpu.HBM)] * 3,
        out_specs=[whole(*dims) for dims in shapes],
        scratch_shapes=[pltpu.VMEM((256, 768), BF16)] * 3 + [pltpu.SemaphoreType.DMA((3,))],
        compiler_params=params(),
        name="prep",
    )(y, queries, keys, values)


def sort_kernel(y_ref, got, away):
    for i in range(3):
        away[i * KV : (i + 1) * KV, :] = got[lax.rem(y_ref[0] + 1 + i, 4)]


def sort(y, got):
    return pl.pallas_call(
        sort_kernel,
        grid=(1,),
        out_shape=shape(3 * KV, 128),
        in_specs=[SMEM, whole(4, KV, 128)],
        out_specs=whole(3 * KV, 128),
        compiler_params=params(),
        cost_estimate=FREE,
        name="sort",
    )(y, got)


def spread_kernel(rows_ref, out):
    rows = rows_ref[...].astype(F32).reshape(16, 4, 8, 128)
    for group in range(4):
        part = rows[:, group]
        kinds = []
        for base in (0, 3):
            kinds += [part[i, base : base + 2] for i in range(16)]
            kinds += [part[i, base + 2 : base + 3] for i in range(16)]
        packed = jnp.concatenate(kinds, axis=0).astype(BF16)
        for x in range(4):
            for core in range(2):
                out[(x * 4 + group) * 2 + core] = packed


def spread(rows):
    return pl.pallas_call(
        spread_kernel,
        grid=(1,),
        out_shape=shape(32, 96, 128),
        in_specs=[whole(16, 32, 128)],
        out_specs=whole(32, 96, 128),
        compiler_params=params(),
        cost_estimate=FREE,
        name="spread",
    )(rows)


def attend(blocks, queries, head, scores, first_peak):
    mine = queries[head * HEAD_DIM : (head + 1) * HEAD_DIM]
    blank = jnp.zeros_like(mine)
    low = jnp.concatenate([mine, blank], axis=0)
    high = jnp.concatenate([blank, mine], axis=0)
    top = None
    for i, (ref, base) in enumerate(blocks):
        if head < 2:
            parts = [(ref[base : base + 256, :], high if head else low)]
        else:
            third = ref[base + 256 : base + 384, :]
            parts = [(third, low), (third, high)]
        at = i * 256
        for rows, side in parts:
            s = jnp.dot(rows, side, preferred_element_type=F32)
            count = s.shape[0]
            scores[at : at + count, :] = s
            at += count
            here = jnp.max(s.reshape(count // 8, 8, 512), axis=0)
            top = here if top is None else jnp.maximum(top, here)
    peak = jnp.max(top, axis=0, keepdims=True)
    if first_peak is not None:
        peak = jnp.maximum(peak, first_peak)
    total = jnp.zeros((8, 512), F32)
    partial_value = jnp.zeros((HEAD_DIM, 512), F32)
    lo = head * HEAD_DIM
    for i, (ref, base) in enumerate(blocks):
        expos = jnp.exp2((scores[i * 256 : (i + 1) * 256, :] - peak) * FACTOR)
        total = total + jnp.sum(expos.reshape(32, 8, 512), axis=0)
        values = jnp.concatenate(
            [
                ref[base + 384 + lo : base + 384 + lo + HEAD_DIM, :],
                ref[base + 576 + lo : base + 576 + lo + HEAD_DIM, :],
            ],
            axis=1,
        )
        partial_value = partial_value + jnp.dot(
            values, expos.astype(BF16), preferred_element_type=F32
        )
    return peak, jnp.sum(total, axis=0, keepdims=True), partial_value


def near_kernel(counts, has_state, is_last, q_ref, *refs):
    refs = list(refs)
    blocks = []
    for count in counts:
        ref = refs.pop(0)
        blocks += [(ref, i * KV) for i in range(count)]
    if has_state:
        old_sum, old_stat = refs.pop(0), refs.pop(0)
    if is_last:
        far_sum, far_stat = refs.pop(0), refs.pop(0)
        out, scores = refs
    else:
        sum_out, stat_out, scores = refs
    queries = jnp.concatenate([q_ref[0], q_ref[1]], axis=1)
    peaks, totals = [], []
    for head in range(OWN):
        rows = slice(head * HEAD_DIM, (head + 1) * HEAD_DIM)
        first_peak = None
        if has_state:
            old_peak = old_stat[head : head + 1, :]
            old_total = old_stat[4 + head : 5 + head, :]
            first_peak = old_peak
        if is_last:
            far_peak = far_stat[head : head + 1, :]
            far_total = far_stat[8 + head : 9 + head, :]
            first_peak = jnp.maximum(old_peak, far_peak)
        peak, total, partial_value = attend(blocks, queries, head, scores.at[head], first_peak)
        if has_state:
            scale = jnp.exp2((old_peak - peak) * FACTOR)
            total = total + old_total * scale
            partial_value = partial_value + old_sum[rows, :] * scale
        if is_last:
            scale = jnp.exp2((far_peak - peak) * FACTOR)
            total = total + far_total * scale
            partial_value = partial_value + far_sum[rows, :] * scale
            result = (partial_value / total).astype(BF16)
            out[0, rows, :] = result[:, 0:256]
            out[1, rows, :] = result[:, 256:512]
        else:
            sum_out[rows, :] = partial_value
            peaks.append(peak)
            totals.append(total)
    if not is_last:
        blank = [jnp.zeros((1, 512), F32)]
        stat_out[...] = jnp.concatenate(peaks + blank + totals + blank, axis=0)


def near(queries, arrays, state=None, far_state=None):
    def along(rows):
        return pl.BlockSpec((rows, 512), lambda i: (0, i))

    counts = tuple(a.shape[0] // KV for a in arrays)
    is_last = far_state is not None
    two = pl.BlockSpec((2, SPAN, 256), lambda i: (i, 0, 0))
    operands = [queries, *arrays]
    in_specs = [two] + [whole(*a.shape) for a in arrays]
    if state is not None:
        operands += state
        in_specs += [along(SPAN), along(8)]
    if is_last:
        operands += far_state
        in_specs += [along(SPAN), along(16)]
        out_shape, out_specs = shape(4, SPAN, 256), two
    else:
        out_shape = [shape(SPAN, 1024, dtype=F32), shape(8, 1024, dtype=F32)]
        out_specs = [along(SPAN), along(8)]
    return pl.pallas_call(
        functools.partial(near_kernel, counts, state is not None, is_last),
        grid=(2,),
        out_shape=out_shape,
        in_specs=in_specs,
        out_specs=out_specs,
        scratch_shapes=[pltpu.VMEM((OWN, sum(counts) * 256, 512), F32)],
        compiler_params=params(),
        name="last" if is_last else "near",
    )(*operands)


def far_kernel(y_ref, q_ref, rows_ref, sum_out, stat_out):
    y = y_ref[0]
    place_r = lax.broadcasted_iota(jnp.int32, (1024, 128), 1)
    place = ((place_r // 2) % 4) * 256 + (place_r % 2) * 128 + y * OWN + place_r // 8
    lane = lax.broadcasted_iota(jnp.int32, (1024, 128), 0)
    pick = jnp.where((place_r < 24) & (lane == place), 1.0, 0.0)
    chosen = jnp.zeros((SPAN, 128), F32)
    for t in range(4):
        chosen = chosen + jnp.dot(
            q_ref[t], pick[t * 256 : (t + 1) * 256].astype(BF16), preferred_element_type=F32
        )
    row_head = lax.broadcasted_iota(jnp.int32, (SPAN, 128), 0) // HEAD_DIM
    r_head = lax.broadcasted_iota(jnp.int32, (SPAN, 128), 1) // 8
    mine = row_head == r_head
    chosen = jnp.where(mine, chosen, 0.0).astype(BF16)
    third = chosen[128:192]
    blank = jnp.zeros_like(third)

    def section(low, high):
        return rows_ref[:, low:high, :].reshape(32 * (high - low), 128)

    keys_a, keys_b = section(0, 32), section(32, 48)
    values_a = section(48, 80).astype(F32).T.astype(BF16)
    values_b = section(80, 96).astype(F32).T.astype(BF16)
    r = lax.broadcasted_iota(jnp.int32, (1, 128), 1)
    there_a, there_b = r < 16, r >= 16
    scores = [
        jnp.where(there, jnp.dot(rows, side, preferred_element_type=F32), BLANK)
        for rows, side, there in (
            (keys_a, chosen[0:128], there_a),
            (keys_b, jnp.concatenate([third, blank], axis=0), there_b),
            (keys_b, jnp.concatenate([blank, third], axis=0), there_b),
        )
    ]
    peak = functools.reduce(
        jnp.maximum, [jnp.max(s, axis=0, keepdims=True) for s in scores]
    )
    total = jnp.zeros((1, 128), F32)
    sums = []
    for s, values, there in zip(
        scores,
        (values_a, values_b[0:64], values_b[64:128]),
        (there_a, there_b, there_b),
    ):
        expos = jnp.where(there, jnp.exp2((s - peak) * FACTOR), 0.0)
        total = total + jnp.sum(expos, axis=0, keepdims=True)
        sums.append(jnp.dot(values, expos.astype(BF16), preferred_element_type=F32))
    partial_value = jnp.concatenate([sums[0], sums[1] + sums[2]], axis=0)
    partial_value = jnp.where(mine, partial_value, 0.0)
    head = lax.broadcasted_iota(jnp.int32, (8, 128), 0)
    r8 = lax.broadcasted_iota(jnp.int32, (8, 128), 1)
    same = (r8 // 8 == head) & (r8 < 24)
    wide = jnp.concatenate(
        [
            partial_value,
            jnp.where(same, peak, 0.0),
            jnp.where(same, total, 0.0),
            jnp.where(same, 1.0, 0.0),
        ],
        axis=0,
    )
    dense = lax.dot_general(
        wide,
        pick,
        (((1,), (1,)), ((), ())),
        precision=lax.Precision.HIGHEST,
        preferred_element_type=F32,
    )
    sum_out[...] = dense[0:SPAN]
    there = dense[SPAN + 16 : SPAN + 24] > 0.5
    stat_out[0:8, :] = jnp.where(there, dense[SPAN : SPAN + 8], BLANK)
    stat_out[8:16, :] = dense[SPAN + 8 : SPAN + 16]


def far(y, queries, rows):
    return pl.pallas_call(
        far_kernel,
        grid=(1,),
        out_shape=[shape(SPAN, 1024, dtype=F32), shape(16, 1024, dtype=F32)],
        in_specs=[SMEM, whole(4, SPAN, 256), whole(32, 96, 128)],
        out_specs=[whole(SPAN, 1024), whole(16, 1024)],
        compiler_params=params(),
        name="far",
    )(y, queries, rows)


def turn_kernel(in_ref, out_ref):
    out_ref[...] = in_ref[...].astype(F32).T.astype(BF16)


def turn(array):
    return pl.pallas_call(
        turn_kernel,
        grid=(1,),
        out_shape=shape(256, 768),
        in_specs=[whole(768, 256)],
        out_specs=whole(256, 768),
        compiler_params=params(),
        name="turn",
    )(array)


def exchange(y, staged):
    got = lax.all_to_all(staged, "y", 0, 0, tiled=True)
    return got.reshape(4 * KV, 128), sort(y, got)


def beside(y, q, all_kv, crossed_own, far_rows):
    q = lax.all_to_all(q, "y", 0, 0, tiled=True)
    q, far_rows = lax.optimization_barrier((q, far_rows))
    far_rows = lax.all_to_all(far_rows, ("zl", "zh"), 0, 0, tiled=True)
    partner_kv = move(all_kv, flip=1)
    partner_own = move(crossed_own, flip=1)
    state = near(q, [all_kv, partner_kv, crossed_own, partner_own])
    far_rows, *state = lax.optimization_barrier((far_rows, *state))
    far_rows = lax.all_to_all(spread(far_rows), ("x", "y", "core"), 0, 0, tiled=True)
    return q, tuple(state), tuple(far(y, q, far_rows))


def branch(y, work, *args):
    def blank(*args):
        return jax.tree.map(lambda a: jnp.zeros(a.shape, a.dtype), jax.eval_shape(work, *args))

    return lax.cond(y[0] < 4, work, blank, *args)


def body(queries, keys, values):
    y = lax.axis_index("y").astype(jnp.int32).reshape(1)
    queries, keys, values = (
        pltpu.with_memory_space_constraint(a, pltpu.HBM) for a in (queries, keys, values)
    )
    far_rows, own_kv, staged, q = prep(y, queries, keys, values)
    crossed_own = move(own_kv, dz=8)
    all_kv, away = branch(y, exchange, y, staged)
    away, crossed_own = lax.optimization_barrier((away, crossed_own))
    crossed = move(away, dz=8)
    q, state, far_state = branch(y, beside, y, q, all_kv, crossed_own, far_rows)
    crossed, state, far_state = lax.optimization_barrier((crossed, state, far_state))
    partner_crossed = move(crossed, flip=1)
    state = near(q, [crossed], state)
    result = near(q, [partner_crossed], state, far_state)
    back = lax.all_to_all(result, "y", 0, 0, tiled=True)
    return turn(back.reshape(HEADS * HEAD_DIM, 256))


def solution(mesh):
    fine = Mesh(mesh.devices.reshape(SIZES), AXES)
    placed = P(AXES, None)
    return jax.shard_map(
        body, mesh=fine, in_specs=(placed,) * 3, out_specs=placed, check_vma=False
    )
```
